256 devices in a mesh: gy: 8 (over z), gx: 32 (over x, y, core).
Axes of the slice: x: 4, y: 4, z: 8, core: 2. Of those that a mesh axis runs over, the one named last changes fastest.
Arguments:
- depth_start: float32 [4, 1024, 4096], P(None, 'gy', 'gx'), may hold values from 0.3 to 0.5
- bed_height: float32 [1024, 4096], P('gy', 'gx'), may hold values from 0 to 4.2
- zone_map: int32 [1024, 4096], P('gy', 'gx'), may hold values from 0 to 15, as said below
- manning: float32 [16], replicated, may hold values from 0.04 to 0.3
- observe: float32 [4, 1024, 4096], P(None, 'gy', 'gx'), may hold values from -90 to 90
Outputs:
- final_depth: float32 [4, 1024, 4096], P(None, 'gy', 'gx')
- grad_start: float32 [4, 1024, 4096], P(None, 'gy', 'gx')
- zone_grad: float32 [16], replicated
The draws below stay inside these ranges and needn't reach their ends.
Inputs may be any that keep to these rules, and one draw needn't show every extreme that they name: `zone_map`: constant on aligned patches of 8 x 8 cells.
All inputs are finite; a program needn't handle non-finite values.
Results may differ from the reference program's by a relative error of at most 0.0003.
Values sent between devices are 32-bit elements; how exact they have to be, the bound alone decides.
A program may use at most 64 MiB of HBM per device.

```python
import math
import jax
import jax.numpy as jnp
from jax import lax

EV = 4
STEPS = 4
ZONES = 16
NR = 1024
NC = 4096


def draw_zone_map(key, part):
    key = jax.random.fold_in(key, 7)
    patches = jax.random.randint(key, (NR // 8 + 1, NC // 8 + 1), 0, ZONES)
    spread = jnp.repeat(jnp.repeat(patches, 8, axis=0), 8, axis=1)
    return spread[:NR, :NC].astype(jnp.int32)


def draw_bed_height(key, part):
    key = jax.random.fold_in(key, 5)
    key_phase, key_speckle = jax.random.split(key)
    phases = jax.random.uniform(key_phase, (2,), jnp.float32, 0.0, 6.2831853)
    row_turn = (jnp.arange(NR, dtype=jnp.int32) % 32).astype(jnp.float32) * (6.2831853 / 32.0)
    col_turn = (jnp.arange(NC, dtype=jnp.int32) % 32).astype(jnp.float32) * (6.2831853 / 32.0)
    smooth = 2.0 + jnp.sin(row_turn + phases[0])[:, None] + jnp.sin(col_turn + phases[1])[None, :]
    speckle = jax.random.uniform(key_speckle, (NR, NC), jnp.float32, 0.0, 0.2)
    return (smooth + speckle).astype(jnp.float32)


def draw_observe(key, part):
    key = jax.random.fold_in(key, 11)
    key_base = jax.random.fold_in(key, 0)
    column_share = jnp.arange(NC, dtype=jnp.float32) / max(NC - 1, 1)
    trend = (1.0 + 2.0 * column_share)[None, None, :]
    values = jnp.clip(jax.random.normal(key_base, (EV, NR, NC), jnp.float32), -5.0, 5.0)
    return (values * trend).astype(jnp.float32)


def shard_levels(rng, extent, cuts, smallest, largest):
    factor_of = 1.0
    for axis_at, shards_of in cuts:
        steps = jax.random.uniform(jax.random.fold_in(jax.random.fold_in(rng, 6), axis_at), (shards_of,), jnp.float32, smallest / len(cuts), largest / len(cuts))
        factor_of = factor_of * jnp.repeat(jnp.exp(steps), extent[axis_at] // shards_of).reshape((-1,) + (1,) * (len(extent) - 1 - axis_at))
    return factor_of


def setup_inputs(seed: int = 0) -> dict:
    seeds = jax.random.split(jax.random.key(seed), 6)
    return {
        "depth_start": jnp.clip(0.3 + 0.19999999 * jax.random.uniform(seeds[0], (EV, NR, NC), jnp.float32) ** shard_levels(seeds[0], (EV, NR, NC), ((1, 8), (2, 32)), -0.2, 0.2), 0.3, 0.5),
        "bed_height": draw_bed_height(jax.random.fold_in(seeds[5], 71), 0),
        "zone_map": draw_zone_map(jax.random.fold_in(seeds[5], 71), 0),
        "manning": jnp.clip(jnp.exp(jax.random.uniform(seeds[3], (ZONES,), jnp.float32, math.log(0.04), math.log(0.3))), 0.04, 0.3),
        "observe": draw_observe(jax.random.fold_in(seeds[5], 71), 0),
    }


gravity = 9.81
time_step = 0.3
spacing = 2.0
centre_weight = 0.7
flux_floor = 0.01

def face_flux(water_depth, depth_next, ground, ground_next, flux, flux_low, flux_high, rough_sq, opened):
    face_depth = 0.5 * (water_depth + depth_next)
    surface_slope = (depth_next + ground_next - water_depth - ground) / spacing
    blended = centre_weight * flux + 0.5 * (1.0 - centre_weight) * (flux_low + flux_high)
    friction = 1.0 + gravity * time_step * rough_sq * jnp.sqrt(flux * flux + flux_floor * flux_floor) * jnp.power(face_depth, -7.0 / 3.0)
    return opened * (blended - gravity * time_step * face_depth * surface_slope) / friction

def rolled_high(values, along_dim):
    zero_rim = jnp.zeros_like(lax.slice_in_dim(values, 0, 1, axis=along_dim))
    return jnp.concatenate([lax.slice_in_dim(values, 1, values.shape[along_dim], axis=along_dim), zero_rim], along_dim)

def rolled_low(values, along_dim):
    zero_rim = jnp.zeros_like(lax.slice_in_dim(values, 0, 1, axis=along_dim))
    return jnp.concatenate([zero_rim, lax.slice_in_dim(values, 0, values.shape[along_dim] - 1, axis=along_dim)], along_dim)

def advance(water_depth, flux_x, flux_y, ground, rough_sq, open_x, open_y):
    new_x = face_flux(water_depth, rolled_high(water_depth, 1), ground, rolled_high(ground, 1), flux_x, rolled_low(flux_x, 1), rolled_high(flux_x, 1), rough_sq, open_x)
    new_y = face_flux(water_depth, rolled_high(water_depth, 0), ground, rolled_high(ground, 0), flux_y, rolled_low(flux_y, 0), rolled_high(flux_y, 0), rough_sq, open_y)
    water_depth = water_depth + time_step / spacing * (rolled_low(new_x, 1) - new_x + rolled_low(new_y, 0) - new_y)
    return (water_depth, new_x, new_y)

def reference(depth_start, bed_height, zone_map, manning, observe):
    open_x = (jnp.arange(NC) < NC - 1).astype(jnp.float32)[None, :]
    open_y = (jnp.arange(NR) < NR - 1).astype(jnp.float32)[:, None]

    def run_event(start_depth, coeffs):
        rough_sq = coeffs[zone_map] ** 2
        water_depth = start_depth
        flux_x = jnp.zeros_like(start_depth)
        flux_y = jnp.zeros_like(start_depth)
        for turn_index in range(STEPS):
            water_depth, flux_x, flux_y = advance(water_depth, flux_x, flux_y, bed_height, rough_sq, open_x, open_y)
        return water_depth

    def per_event(event_pair):
        start_depth, weight = event_pair
        last_depth, pullback = jax.vjp(run_event, start_depth, manning)
        grad_depth, grad_coeffs = pullback(weight)
        return (last_depth, grad_depth, grad_coeffs)
    finals, grads, coeff_grads = lax.map(per_event, (depth_start, observe))
    return (finals, grads, lax.optimization_barrier(jnp.sum(coeff_grads, 0)))
```

```python
import functools

import jax
import jax.numpy as jnp
from jax import lax
from jax.experimental import pallas as pl
from jax.experimental.pallas import tpu as pltpu
from jax.sharding import PartitionSpec as P

STEPS = 4
ZONES = 16
EVENTS = 4
GRAVITY = 9.81
TIME_STEP = 0.3
SPACING = 2.0
CENTRE = 0.7
FLOOR = 0.01

RATE = TIME_STEP / SPACING
ALPHA = RATE * GRAVITY * TIME_STEP / (2.0 * SPACING)
BETA = RATE * ALPHA
SIDE = 0.5 * (1.0 - CENTRE)
POWER = -7.0 / 3.0
FLOOR_SQ = (BETA * FLOOR) ** 2
ROUGH_SCALE = GRAVITY * TIME_STEP * (2.0 * ALPHA) ** (-POWER) / BETA
WALL = 1e20

ROWS = 128
LANES = 128
RIM = 8
EXT = ROWS + 2 * RIM
PAD = 8
TALL = EXT + 2 * PAD
BASE = PAD
WIDE = EVENTS + 1

MESH = pl.DeviceIdType.MESH


def lanes_of(shape):
    return lax.broadcasted_iota(jnp.int32, shape, len(shape) - 1)


def rows_of(shape):
    return lax.broadcasted_iota(jnp.int32, shape, len(shape) - 2)


def roll(value, shift, axis=None):
    axis = value.ndim - 1 if axis is None else axis
    return pltpu.roll(value, shift % value.shape[axis], axis)


def mesh_place():
    gy, gx = lax.axis_index("gy"), lax.axis_index("gx")
    ny, nx = lax.axis_size("gy"), lax.axis_size("gx")
    return gy, gx, ny, nx


def fill_own(manning, depth, bed, zone, observe, ext, msg_left, msg_right):
    own = pl.ds(RIM, ROWS)
    classes = zone[pl.ds(0, ROWS // 8, stride=8), :]
    rough = jnp.zeros(classes.shape, jnp.float32)
    for k in range(ZONES):
        m = manning[k]
        rough = jnp.where(classes == k, m * m * ROUGH_SCALE, rough)
    for i in range(ROWS // 8):
        ext[9, RIM + 8 * i : RIM + 8 * i + 8, :] = jnp.broadcast_to(rough[i : i + 1], (8, LANES))
    for e in range(EVENTS):
        ext[e, own, :] = depth[e] * ALPHA
        ext[EVENTS + e, own, :] = observe[e]
    ext[8, own, :] = bed[...] * ALPHA
    lane = lanes_of((ROWS, LANES))
    slot8 = lane // 8
    left = jnp.zeros((ROWS, LANES), jnp.float32)
    right = jnp.zeros((ROWS, LANES), jnp.float32)
    for q in range(10):
        value = ext[q, own, :]
        right = jnp.where(slot8 == q, roll(value, 8 * q + 8), right)
        for e in range(EVENTS):
            if q < EVENTS and q == e:
                at = 4 * e + 3
            elif EVENTS <= q < 8 and q == EVENTS + e:
                at = 4 * e + 2
            elif q == 8:
                at = 4 * e + 1
            elif q == 9:
                at = 4 * e
            else:
                continue
            left = jnp.where(slot8 == at, roll(value, 8 * at), left)
    msg_left[...] = left
    msg_right[...] = right


def neighbours():
    gy, gx, ny, nx = mesh_place()
    up, down = lax.rem(gy + ny - 1, ny), lax.rem(gy + 1, ny)
    west, east = lax.rem(gx + nx - 1, nx), lax.rem(gx + 1, nx)
    return gy, gx, up, down, west, east


def rim_copies(ext, col_left, col_right, msg_left, msg_right, send, recv):
    gy, gx, up, down, west, east = neighbours()
    plans = [
        (msg_left, col_right.at[pl.ds(RIM, ROWS)], (gy, west)),
        (msg_right, col_left.at[pl.ds(RIM, ROWS)], (gy, east)),
        (ext.at[:, pl.ds(ROWS, RIM)], ext.at[:, pl.ds(0, RIM)], (down, gx)),
        (ext.at[:, pl.ds(RIM, RIM)], ext.at[:, pl.ds(RIM + ROWS, RIM)], (up, gx)),
        (msg_left.at[pl.ds(ROWS - RIM, RIM)], col_right.at[pl.ds(0, RIM)], (down, west)),
        (msg_left.at[pl.ds(0, RIM)], col_right.at[pl.ds(RIM + ROWS, RIM)], (up, west)),
        (msg_right.at[pl.ds(ROWS - RIM, RIM)], col_left.at[pl.ds(0, RIM)], (down, east)),
        (msg_right.at[pl.ds(0, RIM)], col_left.at[pl.ds(RIM + ROWS, RIM)], (up, east)),
    ]
    return [
        pltpu.make_async_remote_copy(
            src_ref=src,
            dst_ref=dst,
            send_sem=send.at[i],
            recv_sem=recv.at[i],
            device_id=to,
            device_id_type=MESH,
        )
        for i, (src, dst, to) in enumerate(plans)
    ]


def greet_neighbours(barrier):
    gy, gx, up, down, west, east = neighbours()
    for to in [
        (gy, west),
        (gy, east),
        (down, gx),
        (up, gx),
        (down, west),
        (up, west),
        (down, east),
        (up, east),
    ]:
        pl.semaphore_signal(barrier, inc=1, device_id=to, device_id_type=MESH)


def exchange_kernel(
    manning, depth, bed, zone, observe, ext, col_left, col_right, msg_left, msg_right, send, recv
):
    barrier = pltpu.get_barrier_semaphore()
    greet_neighbours(barrier)
    fill_own(manning, depth, bed, zone, observe, ext, msg_left, msg_right)
    pl.semaphore_wait(barrier, 8)
    copies = rim_copies(ext, col_left, col_right, msg_left, msg_right, send, recv)
    for copy in copies:
        copy.start()
    for copy in copies:
        copy.wait()


def window_main(own, left, at):
    lane = lanes_of(own.shape)
    return jnp.where(lane < RIM, roll(left, -8 * at), roll(own, RIM))


def window_side(owns, right, at):
    lane = lanes_of(owns[0].shape)
    rolled = {}
    out = roll(right, 24 - 8 * at)
    for e, own in enumerate(owns):
        hit = (lane >= 32 * e) & (lane < 32 * e + 24)
        out = jnp.where(hit, roll(own, 24 + 32 * e), out)
    return out


def build_windows(ext, col_left, col_right, depth, bar, gbx, gby, rough_x, rough_y, ground):
    gy, gx, ny, nx = mesh_place()
    here = pl.ds(BASE, EXT)
    left, right = col_left[...], col_right[...]
    for e in range(EVENTS):
        depth[e, here, :] = window_main(ext[e], left, e)
        bar[e, here, :] = window_main(ext[EVENTS + e], left, EVENTS + e)
    depth[EVENTS, here, :] = window_side([ext[e] for e in range(EVENTS)], right, 3)
    bar[EVENTS, here, :] = window_side([ext[EVENTS + e] for e in range(EVENTS)], right, 2)
    shape = (EXT, LANES)
    lane = lanes_of(shape)
    row = rows_of(shape) + (gy * ROWS - RIM)
    wall_y = (row < 0) | (row >= ny * ROWS - 1)
    for w in range(2):
        if w == 0:
            high = window_main(ext[8], left, 8)
            rough = window_main(ext[9], left, 9)
            column = lane + (gx * LANES - RIM)
        else:
            high = window_side([ext[8]] * EVENTS, right, 1)
            rough = window_side([ext[9]] * EVENTS, right, 0)
            column = lane % 32 + (gx * LANES + 104)
        ground[w, here, :] = high
        gbx[w, here, :] = roll(high, -1) - high
        wall_x = (column < 0) | (column >= nx * LANES - 1)
        rough_x[w, here, :] = jnp.where(wall_x, WALL, rough)
        rough_y[w, here, :] = jnp.where(wall_y, WALL, rough)
    for w in range(2):
        gby[w, here, :] = ground[w, pl.ds(BASE + 1, EXT), :] - ground[w, here, :]


def inverse(x):
    y = pl.reciprocal(x, approx=True)
    return y * (2.0 - x * y)


def power_of(double_depth):
    return jnp.exp2((POWER / 0.6931471805599453) * jnp.log(double_depth))


def face(depth, depth_next, gap, flux, sides, rough, first):
    double = depth + depth_next
    slope = (depth_next - depth) + gap
    drive = double * slope
    p = power_of(double)
    if first:
        drag = rough * p * (BETA * FLOOR)
        push = -drive
    else:
        size = flux * flux + FLOOR_SQ
        drag = rough * p * (size * lax.rsqrt(size))
        push = CENTRE * flux + SIDE * sides - drive
    keep = inverse(1.0 + drag)
    return push * keep, drag, keep


def forward_chunk(t, r0, n, depth, fx, fy, drag_x, drag_y, keep_x, keep_y, gbx, gby, rough_x, rough_y):
    here, above, below = pl.ds(r0, n), pl.ds(r0 - 1, n), pl.ds(r0 + 1, n)
    first = t == 0
    for k in range(WIDE):
        w = k // EVENTS
        d = depth[t, k, here, :]
        if first:
            qx = qy = sx = sy = None
        else:
            qx = fx[t - 1, k, here, :]
            qy = fy[t - 1, k, here, :]
            sx = roll(qx, 1) + roll(qx, -1)
            sy = fy[t - 1, k, above, :] + fy[t - 1, k, below, :]
        nx, wx, kx = face(d, roll(d, -1), gbx[w, here, :], qx, sx, rough_x[w, here, :], first)
        ny, wy, ky = face(d, depth[t, k, below, :], gby[w, here, :], qy, sy, rough_y[w, here, :], first)
        fx[t, k, here, :] = nx
        fy[t, k, here, :] = ny
        drag_x[t, k, here, :] = wx
        drag_y[t, k, here, :] = wy
        keep_x[t, k, here, :] = kx
        keep_y[t, k, here, :] = ky
        depth[t + 1, k, here, :] = d + (roll(nx, 1) - nx) + (fy[t, k, above, :] - ny)


def face_back(bar_new, keep, new, drag, depth, depth_next, gap, flux, first):
    a = bar_new * keep
    term = a * (new * drag)
    both = (-POWER) * term * pl.reciprocal(depth + depth_next, approx=True)
    to_here = both + a * (depth + depth - gap)
    to_next = both - a * (depth_next + depth_next + gap)
    if first:
        return a, term, to_here, to_next, None
    size = flux * flux + FLOOR_SQ
    own = CENTRE * a - term * (flux * pl.reciprocal(size, approx=True))
    return a, term, to_here, to_next, own


def backward_chunk(
    t, r0, n, bar, depth, fx, fy, drag_x, drag_y, keep_x, keep_y, gbx, gby, bar_x, bar_y, side_y, down_y, classes
):
    here, above, below = pl.ds(r0, n), pl.ds(r0 - 1, n), pl.ds(r0 + 1, n)
    first = t == 0
    now, past = t % 2, (t + 1) % 2
    sums = [None, None]
    for k in range(WIDE):
        w = k // EVENTS
        bar_d = bar[past, k, here, :]
        back_x = roll(bar_d, -1) - bar_d
        back_y = bar[past, k, below, :] - bar_d
        if t < STEPS - 1:
            back_x = back_x + bar_x[past, k, here, :]
            back_y = back_y + (
                bar_y[past, k, here, :] + SIDE * (side_y[past, k, above, :] + side_y[past, k, below, :])
            )
        d = depth[t, k, here, :]
        qx = None if first else fx[t - 1, k, here, :]
        qy = None if first else fy[t - 1, k, here, :]
        ax, tx, hx, ex, ox = face_back(
            back_x, keep_x[t, k, here, :], fx[t, k, here, :], drag_x[t, k, here, :], d, roll(d, -1), gbx[w, here, :], qx, first
        )
        ay, ty, hy, ey, oy = face_back(
            back_y, keep_y[t, k, here, :], fy[t, k, here, :], drag_y[t, k, here, :], d, depth[t, k, below, :], gby[w, here, :], qy, first
        )
        sums[w] = tx + ty if sums[w] is None else sums[w] + (tx + ty)
        down_y[k, here, :] = ey
        bar[now, k, here, :] = bar_d + (hx + roll(ex, 1)) + (hy + down_y[k, above, :])
        if not first:
            bar_x[now, k, here, :] = ox + SIDE * (roll(ax, 1) + roll(ax, -1))
            bar_y[now, k, here, :] = oy
            side_y[now, k, here, :] = ay
    for w in range(2):
        if t == STEPS - 1:
            classes[w, here, :] = sums[w]
        else:
            classes[w, here, :] = classes[w, here, :] + sums[w]


def unwindow(mains, side, e):
    lane = lanes_of(mains.shape)
    return jnp.where(lane < 112, roll(mains, -RIM), roll(side, 104 - 32 * e))


def class_rows(manning, zone, classes, out):
    own = pl.ds(BASE + RIM, ROWS)
    main, side = classes[0, own, :], classes[1, own, :]
    lane = lanes_of(main.shape)
    tail = roll(side, 104)
    for e in range(1, EVENTS):
        tail = tail + roll(side, 104 - 32 * e)
    both = jnp.where(lane < 112, roll(main, -RIM), tail)
    kinds = zone[pl.ds(0, ROWS // 8, stride=8), :]
    rows = jnp.concatenate([jnp.sum(both[8 * i : 8 * i + 8], axis=0, keepdims=True) for i in range(ROWS // 8)], axis=0)
    lane8 = lanes_of((8, LANES))
    total = jnp.zeros((8, LANES), jnp.float32)
    for k in range(ZONES):
        part = jnp.where(kinds == k, rows, 0.0)
        s = jnp.sum(part)
        m = manning[k]
        total = jnp.where(lane8 == k, s, total)
    out[...] = total


def steps(kernel_rows, loop):
    for r0 in range(BASE, BASE + EXT, kernel_rows):
        loop(r0, min(kernel_rows, BASE + EXT - r0))


CHUNK = 24


def evolve_kernel(
    manning, zone, ext, col_left, col_right, final, grad, partial,
    depth, bar, gbx, gby, rough_x, rough_y, ground,
    fx, fy, drag_x, drag_y, keep_x, keep_y, bar_x, bar_y, side_y, down_y, classes,
):
    build_windows(ext, col_left, col_right, depth.at[0], bar.at[0], gbx, gby, rough_x, rough_y, ground)
    for t in range(STEPS):
        steps(CHUNK, lambda r0, n: forward_chunk(
            t, r0, n, depth, fx, fy, drag_x, drag_y, keep_x, keep_y, gbx, gby, rough_x, rough_y))
    own = pl.ds(BASE + RIM, ROWS)
    side = depth[STEPS, EVENTS, own, :]
    for e in range(EVENTS):
        final[e] = unwindow(depth[STEPS, e, own, :], side, e) * (1.0 / ALPHA)
    for t in reversed(range(STEPS)):
        steps(CHUNK, lambda r0, n: backward_chunk(
            t, r0, n, bar, depth, fx, fy, drag_x, drag_y, keep_x, keep_y, gbx, gby, bar_x, bar_y, side_y, down_y, classes))
    side = bar[0, EVENTS, own, :]
    for e in range(EVENTS):
        grad[e] = unwindow(bar[0, e, own, :], side, e)
    class_rows(manning, zone, classes, partial)


def sum_kernel(partial, total, slots_y, slots_x, send, recv):
    gy, gx, ny, nx = mesh_place()
    barrier = pltpu.get_barrier_semaphore()
    for off in range(1, ny):
        pl.semaphore_signal(barrier, inc=1, device_id=(lax.rem(gy + off, ny), gx), device_id_type=MESH)
    for off in range(1, nx):
        pl.semaphore_signal(barrier, inc=1, device_id=(gy, lax.rem(gx + off, nx)), device_id_type=MESH)
    pl.semaphore_wait(barrier, ny + nx - 2)
    value = partial[...]
    for stage, (slots, count, me) in enumerate([(slots_y, ny, gy), (slots_x, nx, gx)]):
        slots[me] = value
        copies = []
        for off in range(1, count):
            to = lax.rem(me + off, count)
            copies.append(
                pltpu.make_async_remote_copy(
                    src_ref=slots.at[me],
                    dst_ref=slots.at[me],
                    send_sem=send.at[stage],
                    recv_sem=recv.at[stage],
                    device_id=(to, gx) if stage == 0 else (gy, to),
                    device_id_type=MESH,
                )
            )
        for copy in copies:
            copy.start()
        everything = slots.at[pl.ds(0, count - 1)]
        pltpu.make_async_copy(everything, everything, recv.at[stage]).wait()
        value = slots[0]
        for i in range(1, count):
            value = value + slots[i]
        pltpu.make_async_copy(everything, everything, send.at[stage]).wait()
    total[...] = value


def vmem():
    return pl.BlockSpec(memory_space=pltpu.VMEM)


def smem():
    return pl.BlockSpec(memory_space=pltpu.SMEM)


def f32(*shape):
    return jax.ShapeDtypeStruct(shape, jnp.float32)


LIMIT = 60 * 1024 * 1024


def evolve_scratch():
    big = pltpu.VMEM((STEPS, WIDE, TALL, LANES), jnp.float32)
    pair = pltpu.VMEM((2, WIDE, TALL, LANES), jnp.float32)
    wide = pltpu.VMEM((2, TALL, LANES), jnp.float32)
    return [
        pltpu.VMEM((STEPS + 1, WIDE, TALL, LANES), jnp.float32),
        pair,
        wide, wide, wide, wide, wide,
        big, big, big, big, big, big,
        pair, pair, pair,
        pltpu.VMEM((WIDE, TALL, LANES), jnp.float32),
        wide,
    ]


def body(depth_start, bed_height, zone_map, manning, observe):
    ny, nx = lax.axis_size("gy"), lax.axis_size("gx")
    ext, col_left, col_right = pl.pallas_call(
        exchange_kernel,
        out_shape=(f32(10, EXT, LANES), f32(EXT, LANES), f32(EXT, LANES)),
        in_specs=[smem(), vmem(), vmem(), vmem(), vmem()],
        out_specs=(vmem(), vmem(), vmem()),
        scratch_shapes=[
            pltpu.VMEM((ROWS, LANES), jnp.float32),
            pltpu.VMEM((ROWS, LANES), jnp.float32),
            pltpu.SemaphoreType.DMA((8,)),
            pltpu.SemaphoreType.DMA((8,)),
        ],
        compiler_params=pltpu.CompilerParams(collective_id=0, has_side_effects=True),
        name="exchange",
    )(manning, depth_start, bed_height, zone_map, observe)
    final, grad, partial = pl.pallas_call(
        evolve_kernel,
        out_shape=(f32(EVENTS, ROWS, LANES), f32(EVENTS, ROWS, LANES), f32(8, LANES)),
        in_specs=[smem(), vmem(), vmem(), vmem(), vmem()],
        out_specs=(vmem(), vmem(), vmem()),
        scratch_shapes=evolve_scratch(),
        compiler_params=pltpu.CompilerParams(vmem_limit_bytes=LIMIT),
        name="evolve",
    )(manning, zone_map, ext, col_left, col_right)
    total = pl.pallas_call(
        sum_kernel,
        out_shape=f32(8, LANES),
        in_specs=[vmem()],
        out_specs=vmem(),
        scratch_shapes=[
            pltpu.VMEM((ny, 8, LANES), jnp.float32),
            pltpu.VMEM((nx, 8, LANES), jnp.float32),
            pltpu.SemaphoreType.DMA((2,)),
            pltpu.SemaphoreType.DMA((2,)),
        ],
        compiler_params=pltpu.CompilerParams(collective_id=1, has_side_effects=True),
        name="sum_classes",
    )(partial)
    zone_grad = total[0, :ZONES] * (-2.0 / ALPHA) / manning
    return final, grad, zone_grad


def solution(mesh):
    in_specs = (P(None, "gy", "gx"), P("gy", "gx"), P("gy", "gx"), P(), P(None, "gy", "gx"))
    out_specs = (P(None, "gy", "gx"), P(None, "gy", "gx"), P())
    return jax.shard_map(body, mesh=mesh, in_specs=in_specs, out_specs=out_specs, check_vma=False)
```

```python
import collections
import functools

import jax
import jax.numpy as jnp
from jax import lax
from jax.experimental import pallas as pl
from jax.experimental.pallas import tpu as pltpu
from jax.sharding import PartitionSpec as P

STEPS = 4
ZONES = 16
EVENTS = 4
GRAVITY = 9.81
TIME_STEP = 0.3
SPACING = 2.0
CENTRE = 0.7
FLOOR = 0.01

RATE = TIME_STEP / SPACING
SIDE = 0.5 * (1.0 - CENTRE)
MID = CENTRE / SIDE
ALPHA = RATE * GRAVITY * TIME_STEP / (2.0 * SPACING * SIDE)
BETA = RATE * ALPHA
POWER = -7.0 / 3.0
FLOOR_SQ = (BETA * FLOOR) ** 2
ROUGH_SCALE = GRAVITY * TIME_STEP * (2.0 * ALPHA) ** (-POWER) / (BETA * SIDE)
WALL = 1e20

ROWS = 128
LANES = 128
RIM = 8
EXT = ROWS + 2 * RIM
PAD = 8
TALL = EXT + 2 * PAD
BASE = PAD
WIDE = EVENTS + 1

MESH = pl.DeviceIdType.MESH


def lanes_of(shape):
    return lax.broadcasted_iota(jnp.int32, shape, len(shape) - 1)


def rows_of(shape):
    return lax.broadcasted_iota(jnp.int32, shape, len(shape) - 2)


def roll(value, shift, axis=None):
    axis = value.ndim - 1 if axis is None else axis
    return pltpu.roll(value, shift % value.shape[axis], axis)


def mesh_place():
    gy, gx = lax.axis_index("gy"), lax.axis_index("gx")
    ny, nx = lax.axis_size("gy"), lax.axis_size("gx")
    return gy, gx, ny, nx


def own_copies(depth, bed, zone, observe, ext, zone_here, sems):
    own = pl.ds(RIM, ROWS)
    pairs = [
        (zone, zone_here),
        (bed, ext.at[8, own]),
        (depth, ext.at[pl.ds(0, EVENTS), own]),
        (observe, ext.at[pl.ds(EVENTS, EVENTS), own]),
    ]
    return [pltpu.make_async_copy(src, dst, sems.at[i]) for i, (src, dst) in enumerate(pairs)]


def fill_rough(manning, zone, ext):
    classes = zone[pl.ds(0, ROWS // 8, stride=8), :]
    rough = jnp.zeros(classes.shape, jnp.float32)
    for k in range(ZONES):
        m = manning[k]
        rough = jnp.where(classes == k, m * m * ROUGH_SCALE, rough)
    for i in range(ROWS // 8):
        ext[9, RIM + 8 * i : RIM + 8 * i + 8, :] = jnp.broadcast_to(rough[i : i + 1], (8, LANES))


def pack_rims(ext, msg_left, msg_right):
    def one(i, carry):
        here, own = pl.ds(pl.multiple_of(32 * i, 8), 32), pl.ds(pl.multiple_of(32 * i + RIM, 8), 32)
        slot8 = lanes_of((32, LANES)) // 8
        left = jnp.zeros((32, LANES), jnp.float32)
        right = jnp.zeros((32, LANES), jnp.float32)
        for q in range(10):
            value = ext[q, own, :]
            right = jnp.where(slot8 == q, roll(value, 8 * q + 8), right)
            for e in range(EVENTS):
                at = {e: 4 * e + 3, EVENTS + e: 4 * e + 2, 8: 4 * e + 1, 9: 4 * e}.get(q)
                if at is not None:
                    left = jnp.where(slot8 == at, roll(value, 8 * at), left)
        msg_left[here, :] = left
        msg_right[here, :] = right
        return carry

    lax.fori_loop(0, ROWS // 32, one, 0)


def neighbours():
    gy, gx, ny, nx = mesh_place()
    up, down = lax.rem(gy + ny - 1, ny), lax.rem(gy + 1, ny)
    west, east = lax.rem(gx + nx - 1, nx), lax.rem(gx + 1, nx)
    return gy, gx, up, down, west, east


def rim_copies(ext, col_left, col_right, msg_left, msg_right, send, recv):
    gy, gx, up, down, west, east = neighbours()
    plans = [
        (msg_left, col_right.at[pl.ds(RIM, ROWS)], (gy, west)),
        (msg_right, col_left.at[pl.ds(RIM, ROWS)], (gy, east)),
        (ext.at[:, pl.ds(ROWS, RIM)], ext.at[:, pl.ds(0, RIM)], (down, gx)),
        (ext.at[:, pl.ds(RIM, RIM)], ext.at[:, pl.ds(RIM + ROWS, RIM)], (up, gx)),
        (msg_left.at[pl.ds(ROWS - RIM, RIM)], col_right.at[pl.ds(0, RIM)], (down, west)),
        (msg_left.at[pl.ds(0, RIM)], col_right.at[pl.ds(RIM + ROWS, RIM)], (up, west)),
        (msg_right.at[pl.ds(ROWS - RIM, RIM)], col_left.at[pl.ds(0, RIM)], (down, east)),
        (msg_right.at[pl.ds(0, RIM)], col_left.at[pl.ds(RIM + ROWS, RIM)], (up, east)),
    ]
    return [
        pltpu.make_async_remote_copy(
            src_ref=src,
            dst_ref=dst,
            send_sem=send.at[i],
            recv_sem=recv.at[i],
            device_id=to,
            device_id_type=MESH,
        )
        for i, (src, dst, to) in enumerate(plans)
    ]


def greet_neighbours(barrier):
    gy, gx, up, down, west, east = neighbours()
    for to in [
        (gy, west),
        (gy, east),
        (down, gx),
        (up, gx),
        (down, west),
        (up, west),
        (down, east),
        (up, east),
    ]:
        pl.semaphore_signal(barrier, inc=1, device_id=to, device_id_type=MESH)


def window_main(own, left, at):
    lane = lanes_of(own.shape)
    return jnp.where(lane < RIM, roll(left, -8 * at), roll(own, RIM))


def window_side(owns, right, at):
    lane = lanes_of(owns[0].shape)
    rolled = {}
    out = roll(right, 24 - 8 * at)
    for e, own in enumerate(owns):
        hit = (lane >= 32 * e) & (lane < 32 * e + 24)
        out = jnp.where(hit, roll(own, 24 + 32 * e), out)
    return out


def windows_chunk(r0, n, ext, col_left, col_right, depth, bar, gbx, gby, rough_x, rough_y, ground):
    gy, gx, ny, nx = mesh_place()
    here, at = pl.ds(r0, n), pl.ds(r0 - BASE, n)
    left, right = col_left[at, :], col_right[at, :]
    value = [ext[q, at, :] for q in range(10)]
    for e in range(EVENTS):
        depth[e, here, :] = window_main(value[e], left, e) * ALPHA
        bar[e, here, :] = window_main(value[EVENTS + e], left, EVENTS + e)
    depth[EVENTS, here, :] = window_side(value[:EVENTS], right, 3) * ALPHA
    bar[EVENTS, here, :] = window_side(value[EVENTS:8], right, 2)
    shape = (n, LANES)
    lane = lanes_of(shape)
    row = rows_of(shape) + (gy * ROWS - RIM - BASE + r0)
    wall_y = (row < 0) | (row >= ny * ROWS - 1)
    for w in range(2):
        if w == 0:
            high = window_main(value[8], left, 8)
            rough = window_main(value[9], left, 9)
            column = lane + (gx * LANES - RIM)
        else:
            high = window_side([value[8]] * EVENTS, right, 1)
            rough = window_side([value[9]] * EVENTS, right, 0)
            column = lane % 32 + (gx * LANES + 104)
        high = high * ALPHA
        ground[w, here, :] = high
        gbx[w, here, :] = roll(high, -1) - high
        gby[w, pl.ds(r0 - 8, n), :] = ground[w, pl.ds(r0 - 7, n), :] - ground[w, pl.ds(r0 - 8, n), :]
        wall_x = (column < 0) | (column >= nx * LANES - 1)
        rough_x[w, here, :] = jnp.where(wall_x, WALL, rough)
        rough_y[w, here, :] = jnp.where(wall_y, WALL, rough)


def inverse(x):
    return pl.reciprocal(x, approx=True)


def face(depth, depth_next, gap, flux, sides, rough, first):
    double = depth + depth_next
    slope = (depth_next - depth) + gap
    drive = double * slope
    drag = rough * jnp.exp2((POWER / 0.6931471805599453) * jnp.log(double))
    if first:
        drag = drag * (BETA * FLOOR)
        keep = inverse(drag + 1.0 / SIDE)
        new = keep * (-drive)
    else:
        size = flux * flux + FLOOR_SQ
        turn = lax.rsqrt(size)
        drag = drag * (size * turn)
        keep = inverse(drag + 1.0 / SIDE)
        new = keep * ((MID * flux + sides) - drive)
    term = new * drag
    both = ((-POWER) * term) * inverse(double) - slope
    own = None if first else MID - term * ((flux * turn) * turn)
    return new, keep, term, both + double, both - double, own


def forward_chunk(first, last, t, r0, n, v):
    here, above, below = pl.ds(r0, n), pl.ds(r0 - 1, n), pl.ds(r0 + 1, n)
    for k in range(WIDE):
        w = k // EVENTS
        d = v.depth[t, k, here, :]
        if first:
            qx = qy = sx = sy = None
        else:
            qx = v.fx[t - 1, k, here, :]
            qy = v.fy[t - 1, k, here, :]
            sx = roll(qx, 1) + roll(qx, -1)
            sy = v.fy[t - 1, k, above, :] + v.fy[t - 1, k, below, :]
        nx, kx, zx, hx, ex, ox = face(d, roll(d, -1), v.gbx[w, here, :], qx, sx, v.rough_x[w, here, :], first)
        ny, ky, zy, hy, ey, oy = face(d, v.depth[t, k, below, :], v.gby[w, here, :], qy, sy, v.rough_y[w, here, :], first)
        v.fx[t, k, here, :] = nx
        v.fy[t, k, here, :] = ny
        v.keep_x[t, k, here, :] = kx
        v.keep_y[t, k, here, :] = ky
        v.term_x[t, k, here, :] = zx
        v.term_y[t, k, here, :] = zy
        v.here_x[t, k, here, :] = hx
        v.here_y[t, k, here, :] = hy
        v.next_x[t, k, here, :] = ex
        v.next_y[t, k, here, :] = ey
        if not first:
            v.own_x[t, k, here, :] = ox
            v.own_y[t, k, here, :] = oy
        v.depth[t + 1, k, here, :] = d + (roll(nx, 1) - nx) + (v.fy[t, k, above, :] - ny)


def backward_chunk(first, last, t, r0, n, v):
    here, above, below = pl.ds(r0, n), pl.ds(r0 - 1, n), pl.ds(r0 + 1, n)
    sums = [None, None]
    for k in range(WIDE):
        w = k // EVENTS
        bar_d = v.bar[t + 1, k, here, :]
        back_x = roll(bar_d, -1) - bar_d
        back_y = v.bar[t + 1, k, below, :] - bar_d
        if not last:
            back_x = back_x + v.bar_x[t + 1, k, here, :]
            back_y = back_y + (
                v.bar_y[t + 1, k, here, :] + (v.side_y[t + 1, k, above, :] + v.side_y[t + 1, k, below, :])
            )
        ax = back_x * v.keep_x[t, k, here, :]
        ay = back_y * v.keep_y[t, k, here, :]
        both = ax * v.term_x[t, k, here, :] + ay * v.term_y[t, k, here, :]
        sums[w] = both if sums[w] is None else sums[w] + both
        v.side_y[t, k, here, :] = ay
        if first:
            v.side_x[k, here, :] = ax
            continue
        v.down_y[k, here, :] = ay * v.next_y[t, k, here, :]
        v.bar[t, k, here, :] = (
            bar_d
            + (ax * v.here_x[t, k, here, :] + roll(ax * v.next_x[t, k, here, :], 1))
            + (ay * v.here_y[t, k, here, :] + v.down_y[k, above, :])
        )
        v.bar_x[t, k, here, :] = ax * v.own_x[t, k, here, :] + (roll(ax, 1) + roll(ax, -1))
        v.bar_y[t, k, here, :] = ay * v.own_y[t, k, here, :]
    for w in range(2):
        if last:
            v.classes[w, here, :] = sums[w]
        else:
            v.classes[w, here, :] = v.classes[w, here, :] + sums[w]


def start_chunk(r0, n, v):
    here, above = pl.ds(r0, n), pl.ds(r0 - 1, n)
    for k in range(WIDE):
        ax, ay = v.side_x[k, here, :], v.side_y[0, k, here, :]
        v.down_y[k, here, :] = ay * v.next_y[0, k, here, :]
        v.bar[0, k, here, :] = (
            v.bar[1, k, here, :]
            + (ax * v.here_x[0, k, here, :] + roll(ax * v.next_x[0, k, here, :], 1))
            + (ay * v.here_y[0, k, here, :] + v.down_y[k, above, :])
        )


def unwindow(window, side, e):
    return jnp.where(lanes_of(side.shape) < 112, roll(window, -RIM), roll(side, 104 - 32 * e))


def class_row(manning, zone, classes):
    own = pl.ds(BASE + RIM, ROWS)
    main, side = classes[0, own, :], classes[1, own, :]
    lane = lanes_of(main.shape)
    tail = roll(side, 104)
    for e in range(1, EVENTS):
        tail = tail + roll(side, 104 - 32 * e)
    both = jnp.where(lane < 112, roll(main, -RIM), tail)
    kinds = zone[pl.ds(0, ROWS // 8, stride=8), :]
    rows = jnp.concatenate([jnp.sum(both[8 * i : 8 * i + 8], axis=0, keepdims=True) for i in range(ROWS // 8)], axis=0)
    parts = [jnp.sum(jnp.where(kinds == k, rows, 0.0), axis=0, keepdims=True) for k in range(ZONES)]
    sums = jnp.sum(jnp.concatenate(parts, axis=0), axis=1, keepdims=True)
    square = (ZONES, LANES)
    row = jnp.sum(jnp.where(rows_of(square) == lanes_of(square), sums, 0.0), axis=0, keepdims=True)
    lane1 = lanes_of(row.shape)
    each = jnp.ones(row.shape, jnp.float32)
    for k in range(ZONES):
        each = jnp.where(lane1 == k, manning[k], each)
    return row * (-2.0 / ALPHA) / each


SUB = 24


def chunks(rows, step, sub=None):
    sub = min(sub or rows, rows)

    def one(i, carry):
        for j in range(0, rows, sub):
            step(pl.multiple_of(BASE + i * rows + j, 8), sub)
        return carry

    lax.fori_loop(0, EXT // rows, one, 0)


CHUNK_F = 72
CHUNK_B = 72
CHUNK_W = 48
CHUNK_A = 72


FULL = ("fx", "fy", "keep_x", "keep_y", "term_x", "term_y", "here_x", "here_y", "next_x", "next_y", "own_x", "own_y")
FULL += ("bar_x", "bar_y", "side_y")
PLANE = ("ground", "gbx", "gby", "rough_x", "rough_y", "classes")
NAMES = FULL + PLANE + ("depth", "bar", "side_x", "down_y")
Views = collections.namedtuple("Views", NAMES)


def view_scratch():
    tall = (TALL, LANES)
    shapes = [(STEPS, WIDE) + tall] * len(FULL) + [(2,) + tall] * len(PLANE)
    shapes += [(STEPS + 1, WIDE) + tall] * 2 + [(WIDE,) + tall] * 2
    return [pltpu.VMEM(shape, jnp.float32) for shape in shapes]


def over_steps(low, high, down, run):
    if not LOOP_T:
        for t in reversed(range(low, high)) if down else range(low, high):
            run(t)
        return

    def one(i, carry):
        run(high - 1 - i if down else low + i)
        return carry

    lax.fori_loop(0, high - low, one, 0)


LOOP_T = False


def forward(v, ext, col_left, col_right):
    chunks(CHUNK_W, lambda r0, n: windows_chunk(
        r0, n, ext, col_left, col_right, v.depth.at[0], v.bar.at[STEPS], v.gbx, v.gby, v.rough_x, v.rough_y, v.ground))
    last = pl.ds(BASE + EXT - 8, 8)
    for w in range(2):
        v.gby[w, last, :] = v.ground[w, pl.ds(BASE + EXT - 7, 8), :] - v.ground[w, last, :]
    chunks(CHUNK_F, lambda r0, n: forward_chunk(True, False, 0, r0, n, v))
    over_steps(1, STEPS, False, lambda t: chunks(CHUNK_F, lambda r0, n: forward_chunk(False, False, t, r0, n, v)))


def backward(v):
    chunks(CHUNK_B, lambda r0, n: backward_chunk(False, True, STEPS - 1, r0, n, v))
    over_steps(1, STEPS - 1, True, lambda t: chunks(CHUNK_B, lambda r0, n: backward_chunk(False, False, t, r0, n, v)))
    chunks(CHUNK_A, lambda r0, n: backward_chunk(True, False, 0, r0, n, v))


def stage_of(which):
    gy, gx, ny, nx = mesh_place()
    return (ny, gy) if which == 0 else (nx, gx)


def stage_peers(which):
    gy, gx, ny, nx = mesh_place()
    if which == 0:
        far = sorted(range(1, ny), key=lambda off: -min(off, ny - off))
        return [(lax.rem(gy + off, ny), gx) for off in far]
    if nx % 32:
        return [(gy, lax.rem(gx + off, nx)) for off in range(1, nx)]
    x, y, core = gx // 8, lax.rem(gx // 2, 4), lax.rem(gx, 2)
    xs = [lax.rem(x + d, nx // 8) * 8 for d in range(nx // 8)]
    ys = [lax.rem(y + d, 4) * 2 for d in range(4)]
    cores = [core, 1 - core]
    hops = lambda d, n: min(d, n - d)
    steps = [(dx, dy, dc) for dx in range(nx // 8) for dy in range(4) for dc in range(2)][1:]
    steps.sort(key=lambda d: -(2 * hops(d[0], nx // 8) + 2 * hops(d[1], 4) + d[2]))
    return [(gy, xs[dx] + ys[dy] + cores[dc]) for dx, dy, dc in steps]


def greet_stage(barrier, which):
    for to in stage_peers(which):
        pl.semaphore_signal(barrier, inc=1, device_id=to, device_id_type=MESH)


def send_stage(which, value, slots, send, recv):
    count, me = stage_of(which)
    slots[me] = value
    for to in stage_peers(which):
        pltpu.make_async_remote_copy(
            src_ref=slots.at[me],
            dst_ref=slots.at[me],
            send_sem=send.at[which],
            recv_sem=recv.at[which],
            device_id=to,
            device_id_type=MESH,
        ).start()


def sum_stage(which, slots, recv):
    count, me = stage_of(which)
    others = slots.at[pl.ds(0, count - 1)]
    pltpu.make_async_copy(others, others, recv.at[which]).wait()
    return jnp.sum(slots[...], axis=0)


def drain_stage(which, slots, send):
    count, me = stage_of(which)
    others = slots.at[pl.ds(0, count - 1)]
    pltpu.make_async_copy(others, others, send.at[which]).wait()


def kernel(
    manning, depth, bed, zone, observe, final, grad, total,
    ext, zone_here, col_left, col_right, msg_left, msg_right, slots_y, slots_x,
    own_sems, rim_send, rim_recv, sum_send, sum_recv, out_sems, *views,
):
    v = Views(*views)
    gy, gx, ny, nx = mesh_place()
    barrier = pltpu.get_barrier_semaphore()
    copies = own_copies(depth, bed, zone, observe, ext, zone_here, own_sems)
    for copy in copies:
        copy.start()
    greet_neighbours(barrier)
    greet_stage(barrier, 0)
    greet_stage(barrier, 1)
    for copy in copies:
        copy.wait()
    fill_rough(manning, zone_here, ext)
    pack_rims(ext, msg_left, msg_right)
    pl.semaphore_wait(barrier, 8 + ny - 1 + nx - 1)
    rims = rim_copies(ext, col_left, col_right, msg_left, msg_right, rim_send, rim_recv)
    for copy in rims:
        copy.start()
    for copy in rims:
        copy.wait()
    forward(v, ext, col_left, col_right)
    own = pl.ds(BASE + RIM, ROWS)
    final_copy = pltpu.make_async_copy(v.depth.at[STEPS, :, own], final, out_sems.at[0])
    final_copy.start()
    backward(v)
    send_stage(0, class_row(manning, zone_here, v.classes), slots_y, sum_send, sum_recv)
    chunks(CHUNK_A, lambda r0, n: start_chunk(r0, n, v))
    grad_copy = pltpu.make_async_copy(v.bar.at[0, :, own], grad, out_sems.at[1])
    grad_copy.start()
    send_stage(1, sum_stage(0, slots_y, sum_recv), slots_x, sum_send, sum_recv)
    final_copy.wait()
    drain_stage(0, slots_y, sum_send)
    total[...] = sum_stage(1, slots_x, sum_recv)
    drain_stage(1, slots_x, sum_send)
    grad_copy.wait()


def vmem():
    return pl.BlockSpec(memory_space=pltpu.VMEM)


def smem():
    return pl.BlockSpec(memory_space=pltpu.SMEM)


def f32(*shape):
    return jax.ShapeDtypeStruct(shape, jnp.float32)


LIMIT = 60 * 1024 * 1024


def finish_kernel(final_windows, grad_windows, total, final, grad, zone_grad):
    final_side, grad_side = final_windows[EVENTS], grad_windows[EVENTS]
    for e in range(EVENTS):
        final[e] = unwindow(final_windows[e], final_side, e) * (1.0 / ALPHA)
        grad[e] = unwindow(grad_windows[e], grad_side, e)
    zone_grad[...] = total[0, :ZONES]


def anywhere():
    return pl.BlockSpec(memory_space=pl.ANY)


def body(depth_start, bed_height, zone_map, manning, observe):
    ny, nx = lax.axis_size("gy"), lax.axis_size("gx")
    block = pltpu.VMEM((ROWS, LANES), jnp.float32)
    rim = pltpu.VMEM((EXT, LANES), jnp.float32)
    final_windows, grad_windows, total = pl.pallas_call(
        kernel,
        out_shape=(f32(WIDE, ROWS, LANES), f32(WIDE, ROWS, LANES), f32(1, LANES)),
        in_specs=[smem(), anywhere(), anywhere(), anywhere(), anywhere()],
        out_specs=(anywhere(), anywhere(), vmem()),
        scratch_shapes=[
            pltpu.VMEM((10, EXT, LANES), jnp.float32),
            pltpu.VMEM((ROWS, LANES), jnp.int32),
            rim, rim, block, block,
            pltpu.VMEM((ny, 1, LANES), jnp.float32),
            pltpu.VMEM((nx, 1, LANES), jnp.float32),
            pltpu.SemaphoreType.DMA((4,)),
            pltpu.SemaphoreType.DMA((8,)),
            pltpu.SemaphoreType.DMA((8,)),
            pltpu.SemaphoreType.DMA((2,)),
            pltpu.SemaphoreType.DMA((2,)),
            pltpu.SemaphoreType.DMA((2,)),
        ]
        + view_scratch(),
        compiler_params=pltpu.CompilerParams(collective_id=0, has_side_effects=True, vmem_limit_bytes=LIMIT),
        name="flood",
    )(manning, depth_start, bed_height, zone_map, observe)
    return pl.pallas_call(
        finish_kernel,
        out_shape=(f32(EVENTS, ROWS, LANES), f32(EVENTS, ROWS, LANES), f32(ZONES)),
        in_specs=[vmem(), vmem(), vmem()],
        out_specs=(vmem(), vmem(), vmem()),
        compiler_params=pltpu.CompilerParams(vmem_limit_bytes=LIMIT),
        name="finish",
    )(final_windows, grad_windows, total)


def solution(mesh):
    in_specs = (P(None, "gy", "gx"), P("gy", "gx"), P("gy", "gx"), P(), P(None, "gy", "gx"))
    out_specs = (P(None, "gy", "gx"), P(None, "gy", "gx"), P())
    return jax.shard_map(body, mesh=mesh, in_specs=in_specs, out_specs=out_specs, check_vma=False)
```

```python
import collections
import functools

import jax
import jax.numpy as jnp
from jax import lax
from jax.experimental import pallas as pl
from jax.experimental.pallas import tpu as pltpu
from jax.sharding import PartitionSpec as P

STEPS = 4
ZONES = 16
EVENTS = 4
GRAVITY = 9.81
TIME_STEP = 0.3
SPACING = 2.0
CENTRE = 0.7
FLOOR = 0.01

RATE = TIME_STEP / SPACING
SIDE = 0.5 * (1.0 - CENTRE)
MID = CENTRE / SIDE
ALPHA = RATE * GRAVITY * TIME_STEP / (2.0 * SPACING * SIDE)
BETA = RATE * ALPHA
POWER = -7.0 / 3.0
FLOOR_SQ = (BETA * FLOOR) ** 2
ROUGH_SCALE = GRAVITY * TIME_STEP * (2.0 * ALPHA) ** (-POWER) / (BETA * SIDE)
WALL = 1e20

ROWS = 128
LANES = 128
RIM = 8
EXT = ROWS + 2 * RIM
PAD = 8
TALL = EXT + 2 * PAD
BASE = PAD
WIDE = EVENTS + 1

MESH = pl.DeviceIdType.MESH


def lanes_of(shape):
    return lax.broadcasted_iota(jnp.int32, shape, len(shape) - 1)


def rows_of(shape):
    return lax.broadcasted_iota(jnp.int32, shape, len(shape) - 2)


def roll(value, shift, axis=None):
    axis = value.ndim - 1 if axis is None else axis
    return pltpu.roll(value, shift % value.shape[axis], axis)


def mesh_place():
    gy, gx = lax.axis_index("gy"), lax.axis_index("gx")
    ny, nx = lax.axis_size("gy"), lax.axis_size("gx")
    return gy, gx, ny, nx


def own_copies(depth, bed, zone, observe, ext, zone_here, sems):
    own = pl.ds(RIM, ROWS)
    pairs = [
        (zone, zone_here),
        (bed, ext.at[8, own]),
        (depth, ext.at[pl.ds(0, EVENTS), own]),
        (observe, ext.at[pl.ds(EVENTS, EVENTS), own]),
    ]
    return [pltpu.make_async_copy(src, dst, sems.at[i]) for i, (src, dst) in enumerate(pairs)]


def fill_rough(manning, zone, ext):
    classes = zone[pl.ds(0, ROWS // 8, stride=8), :]
    rough = jnp.zeros(classes.shape, jnp.float32)
    for k in range(ZONES):
        m = manning[k]
        rough = jnp.where(classes == k, m * m * ROUGH_SCALE, rough)
    for i in range(ROWS // 8):
        ext[9, RIM + 8 * i : RIM + 8 * i + 8, :] = jnp.broadcast_to(rough[i : i + 1], (8, LANES))


def pack_rims(ext, msg_left, msg_right):
    def one(i, carry):
        here, own = pl.ds(pl.multiple_of(64 * i, 8), 64), pl.ds(pl.multiple_of(64 * i + RIM, 8), 64)
        slot8 = lanes_of((64, LANES)) // 8
        left = jnp.zeros((64, LANES), jnp.float32)
        right = jnp.zeros((64, LANES), jnp.float32)
        for q in range(10):
            value = scaled(q, ext[q, own, :])
            right = jnp.where(slot8 == q, roll(value, 8 * q + 8), right)
            for e in range(EVENTS):
                at = {e: 4 * e + 3, EVENTS + e: 4 * e + 2, 8: 4 * e + 1, 9: 4 * e}.get(q)
                if at is not None:
                    left = jnp.where(slot8 == at, roll(value, 8 * at), left)
        msg_left[here, :] = left
        msg_right[here, :] = right
        return carry

    lax.fori_loop(0, ROWS // 64, one, 0)


def neighbours():
    gy, gx, ny, nx = mesh_place()
    up, down = lax.rem(gy + ny - 1, ny), lax.rem(gy + 1, ny)
    west, east = lax.rem(gx + nx - 1, nx), lax.rem(gx + 1, nx)
    return gy, gx, up, down, west, east


def rim_copies(ext, col_left, col_right, msg_left, msg_right, send, recv):
    gy, gx, up, down, west, east = neighbours()
    plans = [
        (msg_left.at[pl.ds(ROWS - RIM, RIM)], col_right.at[pl.ds(0, RIM)], (down, west)),
        (msg_left.at[pl.ds(0, RIM)], col_right.at[pl.ds(RIM + ROWS, RIM)], (up, west)),
        (msg_right.at[pl.ds(ROWS - RIM, RIM)], col_left.at[pl.ds(0, RIM)], (down, east)),
        (msg_right.at[pl.ds(0, RIM)], col_left.at[pl.ds(RIM + ROWS, RIM)], (up, east)),
        (msg_left, col_right.at[pl.ds(RIM, ROWS)], (gy, west)),
        (msg_right, col_left.at[pl.ds(RIM, ROWS)], (gy, east)),
        (ext.at[:, pl.ds(ROWS, RIM)], ext.at[:, pl.ds(0, RIM)], (down, gx)),
        (ext.at[:, pl.ds(RIM, RIM)], ext.at[:, pl.ds(RIM + ROWS, RIM)], (up, gx)),
    ]
    return [
        pltpu.make_async_remote_copy(
            src_ref=src,
            dst_ref=dst,
            send_sem=send.at[i],
            recv_sem=recv.at[i],
            device_id=to,
            device_id_type=MESH,
        )
        for i, (src, dst, to) in enumerate(plans)
    ]


def greet_neighbours(barrier):
    gy, gx, up, down, west, east = neighbours()
    for to in [
        (down, west),
        (up, west),
        (down, east),
        (up, east),
        (gy, west),
        (gy, east),
        (down, gx),
        (up, gx),
    ]:
        pl.semaphore_signal(barrier, inc=1, device_id=to, device_id_type=MESH)


def scaled(q, value):
    return value * ALPHA if q < EVENTS or q == 8 else value


def window_side(owns):
    lane = lanes_of(owns[0].shape)
    out = roll(owns[0], 24)
    for e in range(1, EVENTS):
        out = jnp.where(lane >= 32 * e, roll(owns[e], 24 + 32 * e), out)
    return out


def own_windows(ext, at):
    value = [scaled(q, ext[q, at, :]) for q in range(10)]
    mains = [roll(x, RIM) for x in value]
    sides = [window_side(x) for x in (value[:EVENTS], value[EVENTS:8], [value[8]] * EVENTS, [value[9]] * EVENTS)]
    return mains + sides


def window_refs(v):
    first, last = v.depth.at[0], v.bar.at[STEPS]
    mains = [first.at[e] for e in range(EVENTS)] + [last.at[e] for e in range(EVENTS)]
    mains += [v.ground.at[0], v.rough_x.at[0]]
    return mains + [first.at[EVENTS], last.at[EVENTS], v.ground.at[1], v.rough_x.at[1]]


def windows_before(ext, v):
    def one(i, carry):
        r0 = pl.multiple_of(32 * i, 8)
        for ref, value in zip(window_refs(v), own_windows(ext, pl.ds(r0 + RIM, 32))):
            ref[pl.ds(r0 + BASE + RIM, 32), :] = value
        return carry

    lax.fori_loop(0, ROWS // 32, one, 0)


def windows_chunk(r0, n, ext, col_left, col_right, v, own):
    gy, gx, ny, nx = mesh_place()
    here, at = pl.ds(r0, n), pl.ds(r0 - BASE, n)
    left, right = col_left[at, :], col_right[at, :]
    refs = window_refs(v)
    values = [ref[here, :] for ref in refs] if own else own_windows(ext, at)
    lane = lanes_of((n, LANES))
    for q in range(10):
        values[q] = jnp.where(lane < RIM, roll(left, -8 * q), values[q])
    tail = lane % 32 >= 24
    for i in range(4):
        values[10 + i] = jnp.where(tail, roll(right, 8 * i), values[10 + i])
    row = rows_of((n, LANES)) + (gy * ROWS - RIM - BASE + r0)
    wall_y = (row < 0) | (row >= ny * ROWS - 1)
    for ref, value in zip(refs[:9] + refs[10:13], values[:9] + values[10:13]):
        ref[here, :] = value
    for w in range(2):
        ground, rough = (values[8], values[9]) if w == 0 else (values[12], values[13])
        column = lane + (gx * LANES - RIM) if w == 0 else lane % 32 + (gx * LANES + 104)
        wall_x = (column < 0) | (column >= nx * LANES - 1)
        v.gbx[w, here, :] = roll(ground, -1) - ground
        v.rough_x[w, here, :] = jnp.where(wall_x, WALL, rough)
        v.rough_y[w, here, :] = jnp.where(wall_y, WALL, rough)
        if own:
            fall(v, w, r0 - 8, n)


def fall(v, w, r0, n):
    v.gby[w, pl.ds(r0, n), :] = v.ground[w, pl.ds(r0 + 1, n), :] - v.ground[w, pl.ds(r0, n), :]


def windows_after(ext, col_left, col_right, v):
    windows_chunk(BASE, RIM, ext, col_left, col_right, v, False)

    def one(i, carry):
        windows_chunk(pl.multiple_of(32 * i, 8) + BASE + RIM, 32, ext, col_left, col_right, v, True)
        return carry

    lax.fori_loop(0, ROWS // 32, one, 0)
    windows_chunk(BASE + RIM + ROWS, RIM, ext, col_left, col_right, v, False)
    for w in range(2):
        fall(v, w, BASE + EXT - 16, 16)


def inverse(x):
    return pl.reciprocal(x, approx=True)


def face(depth, depth_next, gap, flux, sides, rough, first):
    double = depth + depth_next
    slope = (depth_next - depth) + gap
    drive = double * slope
    drag = rough * jnp.exp2((POWER / 0.6931471805599453) * jnp.log(double))
    if first:
        drag = drag * (BETA * FLOOR)
        keep = inverse(drag + 1.0 / SIDE)
        new = keep * (-drive)
        term = new * drag
        own = None
    else:
        size = flux * flux + FLOOR_SQ
        drag = drag * lax.rsqrt(size)
        keep = inverse(drag * size + 1.0 / SIDE)
        new = keep * ((MID * flux + sides) - drive)
        drag = new * drag
        term = drag * size
        own = MID - drag * flux
    both = ((-POWER) * term) * inverse(double) - slope
    return new, keep, term, both + double, both - double, own


def forward_chunk(first, last, t, r0, n, v):
    here, above, below = pl.ds(r0, n), pl.ds(r0 - 1, n), pl.ds(r0 + 1, n)
    for k in range(WIDE):
        w = k // EVENTS
        d = v.depth[t, k, here, :]
        if first:
            qx = qy = sx = sy = None
        else:
            qx = v.fx[t - 1, k, here, :]
            qy = v.fy[t - 1, k, here, :]
            sx = roll(qx, 1) + roll(qx, -1)
            sy = v.fy[t - 1, k, above, :] + v.fy[t - 1, k, below, :]
        nx, kx, zx, hx, ex, ox = face(d, roll(d, -1), v.gbx[w, here, :], qx, sx, v.rough_x[w, here, :], first)
        ny, ky, zy, hy, ey, oy = face(d, v.depth[t, k, below, :], v.gby[w, here, :], qy, sy, v.rough_y[w, here, :], first)
        v.fx[t, k, here, :] = nx
        v.fy[t, k, here, :] = ny
        v.keep_x[t, k, here, :] = kx
        v.keep_y[t, k, here, :] = ky
        v.term_x[t, k, here, :] = zx
        v.term_y[t, k, here, :] = zy
        v.here_x[t, k, here, :] = hx
        v.here_y[t, k, here, :] = hy
        v.next_x[t, k, here, :] = ex
        v.next_y[t, k, here, :] = ey
        if not first:
            v.own_x[t, k, here, :] = ox
            v.own_y[t, k, here, :] = oy
        v.depth[t + 1, k, here, :] = d + (roll(nx, 1) - nx) + (v.fy[t, k, above, :] - ny)


def backward_chunk(first, last, t, r0, n, v):
    here, above, below = pl.ds(r0, n), pl.ds(r0 - 1, n), pl.ds(r0 + 1, n)
    sums = [None, None]
    for k in range(WIDE):
        w = k // EVENTS
        bar_d = v.bar[t + 1, k, here, :]
        back_y = v.bar[t + 1, k, below, :] - bar_d
        if last:
            back_x = roll(bar_d, -1) - bar_d
        else:
            back_x = v.back_x[t + 1, k, here, :]
            back_y = back_y + (
                v.bar_y[t + 1, k, here, :] + (v.side_y[t + 1, k, above, :] + v.side_y[t + 1, k, below, :])
            )
        ax = back_x * v.keep_x[t, k, here, :]
        ay = back_y * v.keep_y[t, k, here, :]
        both = ax * v.term_x[t, k, here, :] + ay * v.term_y[t, k, here, :]
        sums[w] = both if sums[w] is None else sums[w] + both
        v.side_y[t, k, here, :] = ay
        if first:
            v.side_x[k, here, :] = ax
            continue
        v.down_y[k, here, :] = ay * v.next_y[t, k, here, :]
        base = (bar_d + ax * v.here_x[t, k, here, :]) + (ay * v.here_y[t, k, here, :] + v.down_y[k, above, :])
        right = ax * v.next_x[t, k, here, :]
        v.bar[t, k, here, :] = base + roll(right, 1)
        v.back_x[t, k, here, :] = (roll(base + ax, -1) + roll(ax - right, 1)) + (
            (right + ax * v.own_x[t, k, here, :]) - base
        )
        v.bar_y[t, k, here, :] = ay * v.own_y[t, k, here, :]
    for w in range(2):
        if last:
            v.classes[w, here, :] = sums[w]
        else:
            v.classes[w, here, :] = v.classes[w, here, :] + sums[w]


def start_chunk(r0, n, v):
    here, above = pl.ds(r0, n), pl.ds(r0 - 1, n)
    for k in range(WIDE):
        ax, ay = v.side_x[k, here, :], v.side_y[0, k, here, :]
        v.down_y[k, here, :] = ay * v.next_y[0, k, here, :]
        v.bar[0, k, here, :] = (
            v.bar[1, k, here, :]
            + (ax * v.here_x[0, k, here, :] + roll(ax * v.next_x[0, k, here, :], 1))
            + (ay * v.here_y[0, k, here, :] + v.down_y[k, above, :])
        )


def unwindow(source, target, scale):
    def one(i, carry):
        at = pl.ds(pl.multiple_of(64 * i, 8), 64)
        here = pl.ds(pl.multiple_of(64 * i, 8) + BASE + RIM, 64)
        side = source[EVENTS, here, :]
        lane = lanes_of(side.shape)
        for e in range(EVENTS):
            own = jnp.where(lane < 112, roll(source[e, here, :], -RIM), roll(side, 104 - 32 * e))
            target[e, at, :] = own if scale is None else own * scale
        return carry

    lax.fori_loop(0, ROWS // 64, one, 0)


def class_row(manning, zone, classes):
    own = pl.ds(BASE + RIM, ROWS)
    main, side = classes[0, own, :], classes[1, own, :]
    lane = lanes_of(main.shape)
    tail = roll(side, 104)
    for e in range(1, EVENTS):
        tail = tail + roll(side, 104 - 32 * e)
    both = jnp.where(lane < 112, roll(main, -RIM), tail)
    kinds = zone[pl.ds(0, ROWS // 8, stride=8), :]
    rows = jnp.concatenate([jnp.sum(both[8 * i : 8 * i + 8], axis=0, keepdims=True) for i in range(ROWS // 8)], axis=0)
    parts = [jnp.sum(jnp.where(kinds == k, rows, 0.0), axis=0, keepdims=True) for k in range(ZONES)]
    sums = jnp.sum(jnp.concatenate(parts, axis=0), axis=1, keepdims=True)
    square = (ZONES, LANES)
    row = jnp.sum(jnp.where(rows_of(square) == lanes_of(square), sums, 0.0), axis=0, keepdims=True)
    lane1 = lanes_of(row.shape)
    each = jnp.ones(row.shape, jnp.float32)
    for k in range(ZONES):
        each = jnp.where(lane1 == k, manning[k], each)
    return row * (-2.0 / ALPHA) / each


SUB = 24


def chunks(rows, step, sub=None):
    sub = min(sub or rows, rows)

    def one(i, carry):
        for j in range(0, rows, sub):
            step(pl.multiple_of(BASE + i * rows + j, 8), sub)
        return carry

    lax.fori_loop(0, EXT // rows, one, 0)


CHUNK_F = 72
CHUNK_B = 144
CHUNK_W = 48
CHUNK_A = 72


FULL = ("fx", "fy", "keep_x", "keep_y", "term_x", "term_y", "here_x", "here_y", "next_x", "next_y", "own_x", "own_y")
FULL += ("back_x", "bar_y", "side_y")
PLANE = ("ground", "gbx", "gby", "rough_x", "rough_y", "classes")
NAMES = FULL + PLANE + ("depth", "bar", "side_x", "down_y")
Views = collections.namedtuple("Views", NAMES)


def view_scratch():
    tall = (TALL, LANES)
    shapes = [(STEPS, WIDE) + tall] * len(FULL) + [(2,) + tall] * len(PLANE)
    shapes += [(STEPS + 1, WIDE) + tall] * 2 + [(WIDE,) + tall] * 2
    return [pltpu.VMEM(shape, jnp.float32) for shape in shapes]


def over_steps(low, high, down, run):
    if not LOOP_T:
        for t in reversed(range(low, high)) if down else range(low, high):
            run(t)
        return

    def one(i, carry):
        run(high - 1 - i if down else low + i)
        return carry

    lax.fori_loop(0, high - low, one, 0)


LOOP_T = False


def forward(v):
    chunks(CHUNK_F, lambda r0, n: forward_chunk(True, False, 0, r0, n, v))
    over_steps(1, STEPS, False, lambda t: chunks(CHUNK_F, lambda r0, n: forward_chunk(False, False, t, r0, n, v)))


def backward(v):
    chunks(CHUNK_B, lambda r0, n: backward_chunk(False, True, STEPS - 1, r0, n, v))
    over_steps(1, STEPS - 1, True, lambda t: chunks(CHUNK_B, lambda r0, n: backward_chunk(False, False, t, r0, n, v)))
    chunks(CHUNK_A, lambda r0, n: backward_chunk(True, False, 0, r0, n, v))


def stage_of(which):
    gy, gx, ny, nx = mesh_place()
    return (ny, gy) if which == 0 else (nx, gx)


def stage_peers(which):
    gy, gx, ny, nx = mesh_place()
    if which == 0:
        far = sorted(range(1, ny), key=lambda off: -min(off, ny - off))
        return [(lax.rem(gy + off, ny), gx) for off in far]
    if nx % 32:
        return [(gy, lax.rem(gx + off, nx)) for off in range(1, nx)]
    x, y, core = gx // 8, lax.rem(gx // 2, 4), lax.rem(gx, 2)
    xs = [lax.rem(x + d, nx // 8) * 8 for d in range(nx // 8)]
    ys = [lax.rem(y + d, 4) * 2 for d in range(4)]
    cores = [core, 1 - core]
    hops = lambda d, n: min(d, n - d)
    steps = [(dx, dy, dc) for dx in range(nx // 8) for dy in range(4) for dc in range(2)][1:]
    steps.sort(key=lambda d: -(2 * hops(d[0], nx // 8) + 2 * hops(d[1], 4) + d[2]))
    return [(gy, xs[dx] + ys[dy] + cores[dc]) for dx, dy, dc in steps]


def greet_stage(barrier, which):
    for to in stage_peers(which):
        pl.semaphore_signal(barrier, inc=1, device_id=to, device_id_type=MESH)


def send_stage(which, value, slots, send, recv):
    count, me = stage_of(which)
    slots[me] = value
    for to in stage_peers(which):
        pltpu.make_async_remote_copy(
            src_ref=slots.at[me],
            dst_ref=slots.at[me],
            send_sem=send.at[which],
            recv_sem=recv.at[which],
            device_id=to,
            device_id_type=MESH,
        ).start()


def sum_stage(which, slots, recv):
    count, me = stage_of(which)
    others = slots.at[pl.ds(0, count - 1)]
    pltpu.make_async_copy(others, others, recv.at[which]).wait()
    return jnp.sum(slots[...], axis=0)


def drain_stage(which, slots, send):
    count, me = stage_of(which)
    others = slots.at[pl.ds(0, count - 1)]
    pltpu.make_async_copy(others, others, send.at[which]).wait()


def kernel(
    manning, depth, bed, zone, observe, final, grad, total,
    ext, zone_here, col_left, col_right, msg_left, msg_right, final_here, grad_here, slots_y, slots_x,
    own_sems, rim_send, rim_recv, sum_send, sum_recv, out_sems, *views,
):
    v = Views(*views)
    gy, gx, ny, nx = mesh_place()
    barrier = pltpu.get_barrier_semaphore()
    copies = own_copies(depth, bed, zone, observe, ext, zone_here, own_sems)
    greet_neighbours(barrier)
    for copy in copies:
        copy.start()
    greet_stage(barrier, 0)
    greet_stage(barrier, 1)
    for copy in copies:
        copy.wait()
    fill_rough(manning, zone_here, ext)
    pack_rims(ext, msg_left, msg_right)
    pl.semaphore_wait(barrier, 8 + ny - 1 + nx - 1)
    rims = rim_copies(ext, col_left, col_right, msg_left, msg_right, rim_send, rim_recv)
    for copy in rims:
        copy.start()
    windows_before(ext, v)
    for copy in rims:
        copy.wait()
    windows_after(ext, col_left, col_right, v)
    forward(v)
    backward(v)
    send_stage(0, class_row(manning, zone_here, v.classes), slots_y, sum_send, sum_recv)
    chunks(CHUNK_A, lambda r0, n: start_chunk(r0, n, v))
    unwindow(v.bar.at[0], grad_here, None)
    grad_copy = pltpu.make_async_copy(grad_here, grad, out_sems.at[0])
    grad_copy.start()
    unwindow(v.depth.at[STEPS], final_here, 1.0 / ALPHA)
    final_copy = pltpu.make_async_copy(final_here, final, out_sems.at[1])
    final_copy.start()
    send_stage(1, sum_stage(0, slots_y, sum_recv), slots_x, sum_send, sum_recv)
    grad_copy.wait()
    final_copy.wait()
    drain_stage(0, slots_y, sum_send)
    total[...] = sum_stage(1, slots_x, sum_recv)[0, :ZONES]
    drain_stage(1, slots_x, sum_send)


def vmem():
    return pl.BlockSpec(memory_space=pltpu.VMEM)


def smem():
    return pl.BlockSpec(memory_space=pltpu.SMEM)


def f32(*shape):
    return jax.ShapeDtypeStruct(shape, jnp.float32)


LIMIT = 60 * 1024 * 1024


def finish_kernel(final_here, grad_here, sums_here, final, grad, sums):
    final[...] = final_here[...]
    grad[...] = grad_here[...]
    sums[...] = sums_here[...]


def anywhere():
    return pl.BlockSpec(memory_space=pl.ANY)


def body(depth_start, bed_height, zone_map, manning, observe):
    ny, nx = lax.axis_size("gy"), lax.axis_size("gx")
    block = pltpu.VMEM((ROWS, LANES), jnp.float32)
    blocks = pltpu.VMEM((EVENTS, ROWS, LANES), jnp.float32)
    rim = pltpu.VMEM((EXT, LANES), jnp.float32)
    final, grad, sums = pl.pallas_call(
        kernel,
        out_shape=(f32(EVENTS, ROWS, LANES), f32(EVENTS, ROWS, LANES), f32(ZONES)),
        in_specs=[smem(), anywhere(), anywhere(), anywhere(), anywhere()],
        out_specs=(anywhere(), anywhere(), vmem()),
        scratch_shapes=[
            pltpu.VMEM((10, EXT, LANES), jnp.float32),
            pltpu.VMEM((ROWS, LANES), jnp.int32),
            rim, rim, block, block, blocks, blocks,
            pltpu.VMEM((ny, 1, LANES), jnp.float32),
            pltpu.VMEM((nx, 1, LANES), jnp.float32),
            pltpu.SemaphoreType.DMA((4,)),
            pltpu.SemaphoreType.DMA((8,)),
            pltpu.SemaphoreType.DMA((8,)),
            pltpu.SemaphoreType.DMA((2,)),
            pltpu.SemaphoreType.DMA((2,)),
            pltpu.SemaphoreType.DMA((2,)),
        ]
        + view_scratch(),
        compiler_params=pltpu.CompilerParams(collective_id=0, has_side_effects=True, vmem_limit_bytes=LIMIT),
        name="flood",
    )(manning, depth_start, bed_height, zone_map, observe)
    return pl.pallas_call(
        finish_kernel,
        out_shape=(f32(EVENTS, ROWS, LANES), f32(EVENTS, ROWS, LANES), f32(ZONES)),
        in_specs=[vmem(), vmem(), vmem()],
        out_specs=(vmem(), vmem(), vmem()),
        compiler_params=pltpu.CompilerParams(vmem_limit_bytes=LIMIT),
        name="finish",
    )(final, grad, sums)


def solution(mesh):
    in_specs = (P(None, "gy", "gx"), P("gy", "gx"), P("gy", "gx"), P(), P(None, "gy", "gx"))
    out_specs = (P(None, "gy", "gx"), P(None, "gy", "gx"), P())
    return jax.shard_map(body, mesh=mesh, in_specs=in_specs, out_specs=out_specs, check_vma=False)
```

```python
import collections
import functools

import jax
import jax.numpy as jnp
from jax import lax
from jax.experimental import pallas as pl
from jax.experimental.pallas import tpu as pltpu
from jax.sharding import PartitionSpec as P

STEPS = 4
ZONES = 16
EVENTS = 4
GRAVITY = 9.81
TIME_STEP = 0.3
SPACING = 2.0
CENTRE = 0.7
FLOOR = 0.01

RATE = TIME_STEP / SPACING
SIDE = 0.5 * (1.0 - CENTRE)
MID = CENTRE / SIDE
ALPHA = RATE * GRAVITY * TIME_STEP / (2.0 * SPACING * SIDE)
BETA = RATE * ALPHA
POWER = -7.0 / 3.0
FLOOR_SQ = (BETA * FLOOR) ** 2
ROUGH_SCALE = GRAVITY * TIME_STEP * (2.0 * ALPHA) ** (-POWER) / (BETA * SIDE)
WALL = 1e20

ROWS = 128
LANES = 128
RIM = 8
EXT = ROWS + 2 * RIM
PAD = 8
TALL = EXT + 2 * PAD
BASE = PAD
WIDE = EVENTS + 1

MESH = pl.DeviceIdType.MESH


def lanes_of(shape):
    return lax.broadcasted_iota(jnp.int32, shape, len(shape) - 1)


def rows_of(shape):
    return lax.broadcasted_iota(jnp.int32, shape, len(shape) - 2)


def roll(value, shift, axis=None):
    axis = value.ndim - 1 if axis is None else axis
    return pltpu.roll(value, shift % value.shape[axis], axis)


def mesh_place():
    gy, gx = lax.axis_index("gy"), lax.axis_index("gx")
    ny, nx = lax.axis_size("gy"), lax.axis_size("gx")
    return gy, gx, ny, nx


def own_copies(depth, bed, zone, observe, ext, zone_here, sems):
    own = pl.ds(RIM, ROWS)
    pairs = [
        (zone, zone_here),
        (bed, ext.at[8, own]),
        (depth, ext.at[pl.ds(0, EVENTS), own]),
        (observe, ext.at[pl.ds(EVENTS, EVENTS), own]),
    ]
    return [pltpu.make_async_copy(src, dst, sems.at[i]) for i, (src, dst) in enumerate(pairs)]


def fill_rough(manning, zone, ext):
    classes = zone[pl.ds(0, ROWS // 8, stride=8), :]
    rough = jnp.zeros(classes.shape, jnp.float32)
    for k in range(ZONES):
        m = manning[k]
        rough = jnp.where(classes == k, m * m * ROUGH_SCALE, rough)
    for i in range(ROWS // 8):
        ext[9, RIM + 8 * i : RIM + 8 * i + 8, :] = jnp.broadcast_to(rough[i : i + 1], (8, LANES))


def pack_rims(ext, msg_left, msg_right):
    def one(i, carry):
        here, own = pl.ds(pl.multiple_of(128 * i, 8), 128), pl.ds(pl.multiple_of(128 * i + RIM, 8), 128)
        slot8 = lanes_of((128, LANES)) // 8
        left = jnp.zeros((128, LANES), jnp.float32)
        right = jnp.zeros((128, LANES), jnp.float32)
        for q in range(10):
            value = scaled(q, ext[q, own, :])
            right = jnp.where(slot8 == q, roll(value, 8 * q + 8), right)
            for e in range(EVENTS):
                at = {e: 4 * e + 3, EVENTS + e: 4 * e + 2, 8: 4 * e + 1, 9: 4 * e}.get(q)
                if at is not None:
                    left = jnp.where(slot8 == at, roll(value, 8 * at), left)
        msg_left[here, :] = left
        msg_right[here, :] = right
        return carry

    lax.fori_loop(0, ROWS // 128, one, 0)


def neighbours():
    gy, gx, ny, nx = mesh_place()
    up, down = lax.rem(gy + ny - 1, ny), lax.rem(gy + 1, ny)
    west, east = lax.rem(gx + nx - 1, nx), lax.rem(gx + 1, nx)
    return gy, gx, up, down, west, east


def rim_copies(ext, col_left, col_right, msg_left, msg_right, send, recv):
    gy, gx, up, down, west, east = neighbours()
    plans = [
        (msg_left.at[pl.ds(ROWS - RIM, RIM)], col_right.at[pl.ds(0, RIM)], (down, west)),
        (msg_left.at[pl.ds(0, RIM)], col_right.at[pl.ds(RIM + ROWS, RIM)], (up, west)),
        (msg_right.at[pl.ds(ROWS - RIM, RIM)], col_left.at[pl.ds(0, RIM)], (down, east)),
        (msg_right.at[pl.ds(0, RIM)], col_left.at[pl.ds(RIM + ROWS, RIM)], (up, east)),
        (msg_left, col_right.at[pl.ds(RIM, ROWS)], (gy, west)),
        (msg_right, col_left.at[pl.ds(RIM, ROWS)], (gy, east)),
        (ext.at[:, pl.ds(ROWS, RIM)], ext.at[:, pl.ds(0, RIM)], (down, gx)),
        (ext.at[:, pl.ds(RIM, RIM)], ext.at[:, pl.ds(RIM + ROWS, RIM)], (up, gx)),
    ]
    return [
        pltpu.make_async_remote_copy(
            src_ref=src,
            dst_ref=dst,
            send_sem=send.at[i],
            recv_sem=recv.at[i],
            device_id=to,
            device_id_type=MESH,
        )
        for i, (src, dst, to) in enumerate(plans)
    ]


def greet_neighbours(barrier):
    gy, gx, up, down, west, east = neighbours()
    for to in [
        (down, west),
        (up, west),
        (down, east),
        (up, east),
        (gy, west),
        (gy, east),
        (down, gx),
        (up, gx),
    ]:
        pl.semaphore_signal(barrier, inc=1, device_id=to, device_id_type=MESH)


def scaled(q, value):
    return value * ALPHA if q < EVENTS or q == 8 else value


def window_side(owns):
    lane = lanes_of(owns[0].shape)
    out = roll(owns[0], 24)
    for e in range(1, EVENTS):
        out = jnp.where(lane >= 32 * e, roll(owns[e], 24 + 32 * e), out)
    return out


def own_windows(ext, at):
    value = [scaled(q, ext[q, at, :]) for q in range(10)]
    mains = [roll(x, RIM) for x in value]
    sides = [window_side(x) for x in (value[:EVENTS], value[EVENTS:8], [value[8]] * EVENTS, [value[9]] * EVENTS)]
    return mains + sides


def window_refs(v):
    first, last = v.depth.at[0], v.bar.at[STEPS]
    mains = [first.at[e] for e in range(EVENTS)] + [last.at[e] for e in range(EVENTS)]
    mains += [v.ground.at[0], v.rough_x.at[0]]
    return mains + [first.at[EVENTS], last.at[EVENTS], v.ground.at[1], v.rough_x.at[1]]


def windows_before(ext, v):
    def one(i, carry):
        r0 = pl.multiple_of(128 * i, 8)
        for ref, value in zip(window_refs(v), own_windows(ext, pl.ds(r0 + RIM, 128))):
            ref[pl.ds(r0 + BASE + RIM, 128), :] = value
        return carry

    lax.fori_loop(0, ROWS // 128, one, 0)


def windows_chunk(r0, n, ext, col_left, col_right, v, own):
    gy, gx, ny, nx = mesh_place()
    here, at = pl.ds(r0, n), pl.ds(r0 - BASE, n)
    left, right = col_left[at, :], col_right[at, :]
    refs = window_refs(v)
    values = [ref[here, :] for ref in refs] if own else own_windows(ext, at)
    lane = lanes_of((n, LANES))
    for q in range(10):
        values[q] = jnp.where(lane < RIM, roll(left, -8 * q), values[q])
    tail = lane % 32 >= 24
    for i in range(4):
        values[10 + i] = jnp.where(tail, roll(right, 8 * i), values[10 + i])
    row = rows_of((n, LANES)) + (gy * ROWS - RIM - BASE + r0)
    wall_y = (row < 0) | (row >= ny * ROWS - 1)
    for ref, value in zip(refs[:9] + refs[10:13], values[:9] + values[10:13]):
        ref[here, :] = value
    for w in range(2):
        ground, rough = (values[8], values[9]) if w == 0 else (values[12], values[13])
        column = lane + (gx * LANES - RIM) if w == 0 else lane % 32 + (gx * LANES + 104)
        wall_x = (column < 0) | (column >= nx * LANES - 1)
        v.gbx[w, here, :] = roll(ground, -1) - ground
        v.rough_x[w, here, :] = jnp.where(wall_x, WALL, rough)
        v.rough_y[w, here, :] = jnp.where(wall_y, WALL, rough)
        if own:
            fall(v, w, r0 - 8, n)


def fall(v, w, r0, n):
    v.gby[w, pl.ds(r0, n), :] = v.ground[w, pl.ds(r0 + 1, n), :] - v.ground[w, pl.ds(r0, n), :]


def windows_after(ext, col_left, col_right, v):
    windows_chunk(BASE, RIM, ext, col_left, col_right, v, False)

    windows_chunk(BASE + RIM, ROWS, ext, col_left, col_right, v, True)
    windows_chunk(BASE + RIM + ROWS, RIM, ext, col_left, col_right, v, False)
    for w in range(2):
        fall(v, w, BASE + EXT - 16, 16)


def inverse(x):
    return pl.reciprocal(x, approx=True)


def face(depth, depth_next, gap, flux, sides, rough, first):
    double = depth + depth_next
    slope = (depth_next - depth) + gap
    drive = double * slope
    drag = rough * jnp.exp2(POWER * jnp.log2(double))
    if first:
        drag = drag * (BETA * FLOOR)
        keep = inverse(drag + 1.0 / SIDE)
        new = keep * (-drive)
        term = new * drag
        own = None
    else:
        size = flux * flux + FLOOR_SQ
        drag = drag * lax.rsqrt(size)
        keep = inverse(drag * size + 1.0 / SIDE)
        new = keep * ((MID * flux + sides) - drive)
        drag = new * drag
        term = drag * size
        own = MID - drag * flux
    both = ((-POWER) * term) * inverse(double) - slope
    return new, keep, term, both + double, both - double, own


def forward_chunk(first, last, t, r0, n, v):
    here, above, below = pl.ds(r0, n), pl.ds(r0 - 1, n), pl.ds(r0 + 1, n)
    for k in range(WIDE):
        w = k // EVENTS
        d = v.depth[t, k, here, :]
        if first:
            qx = qy = sx = sy = None
        else:
            qx = v.fx[t - 1, k, here, :]
            qy = v.fy[t - 1, k, here, :]
            sx = roll(qx, 1) + roll(qx, -1)
            sy = v.fy[t - 1, k, above, :] + v.fy[t - 1, k, below, :]
        nx, kx, zx, hx, ex, ox = face(d, roll(d, -1), v.gbx[w, here, :], qx, sx, v.rough_x[w, here, :], first)
        ny, ky, zy, hy, ey, oy = face(d, v.depth[t, k, below, :], v.gby[w, here, :], qy, sy, v.rough_y[w, here, :], first)
        v.fx[t, k, here, :] = nx
        v.fy[t, k, here, :] = ny
        v.keep_x[t, k, here, :] = kx
        v.keep_y[t, k, here, :] = ky
        v.term_x[t, k, here, :] = zx
        v.term_y[t, k, here, :] = zy
        v.here_x[t, k, here, :] = hx
        v.here_y[t, k, here, :] = hy
        v.next_x[t, k, here, :] = ex
        v.next_y[t, k, here, :] = ey
        if not first:
            v.own_x[t, k, here, :] = ox
            v.own_y[t, k, here, :] = oy
        v.depth[t + 1, k, here, :] = d + (roll(nx, 1) - nx) + (v.fy[t, k, above, :] - ny)


def backward_chunk(first, last, t, r0, n, v):
    here, above, below = pl.ds(r0, n), pl.ds(r0 - 1, n), pl.ds(r0 + 1, n)
    sums = [None, None]
    for k in range(WIDE):
        w = k // EVENTS
        bar_d = v.bar[t + 1, k, here, :]
        back_y = v.bar[t + 1, k, below, :] - bar_d
        if last:
            back_x = roll(bar_d, -1) - bar_d
        else:
            back_x = v.back_x[t + 1, k, here, :]
            back_y = back_y + (
                v.bar_y[t + 1, k, here, :] + (v.side_y[t + 1, k, above, :] + v.side_y[t + 1, k, below, :])
            )
        ax = back_x * v.keep_x[t, k, here, :]
        ay = back_y * v.keep_y[t, k, here, :]
        both = ax * v.term_x[t, k, here, :] + ay * v.term_y[t, k, here, :]
        sums[w] = both if sums[w] is None else sums[w] + both
        v.side_y[t, k, here, :] = ay
        if first:
            v.side_x[k, here, :] = ax
            continue
        v.down_y[k, here, :] = ay * v.next_y[t, k, here, :]
        base = (bar_d + ax * v.here_x[t, k, here, :]) + (ay * v.here_y[t, k, here, :] + v.down_y[k, above, :])
        right = ax * v.next_x[t, k, here, :]
        v.bar[t, k, here, :] = base + roll(right, 1)
        v.back_x[t, k, here, :] = (roll(base + ax, -1) + roll(ax - right, 1)) + (
            (right + ax * v.own_x[t, k, here, :]) - base
        )
        v.bar_y[t, k, here, :] = ay * v.own_y[t, k, here, :]
    for w in range(2):
        if last:
            v.classes[w, here, :] = sums[w]
        else:
            v.classes[w, here, :] = v.classes[w, here, :] + sums[w]


def start_chunk(r0, n, v):
    here, above = pl.ds(r0, n), pl.ds(r0 - 1, n)
    for k in range(WIDE):
        ax, ay = v.side_x[k, here, :], v.side_y[0, k, here, :]
        v.down_y[k, here, :] = ay * v.next_y[0, k, here, :]
        v.bar[0, k, here, :] = (
            v.bar[1, k, here, :]
            + (ax * v.here_x[0, k, here, :] + roll(ax * v.next_x[0, k, here, :], 1))
            + (ay * v.here_y[0, k, here, :] + v.down_y[k, above, :])
        )


def unwindow(source, target, scale):
    def one(i, carry):
        at = pl.ds(pl.multiple_of(64 * i, 8), 64)
        here = pl.ds(pl.multiple_of(64 * i, 8) + BASE + RIM, 64)
        side = source[EVENTS, here, :]
        lane = lanes_of(side.shape)
        for e in range(EVENTS):
            own = jnp.where(lane < 112, roll(source[e, here, :], -RIM), roll(side, 104 - 32 * e))
            target[e, at, :] = own if scale is None else own * scale
        return carry

    lax.fori_loop(0, ROWS // 64, one, 0)


def class_row(manning, zone, classes):
    own = pl.ds(BASE + RIM, ROWS)
    main, side = classes[0, own, :], classes[1, own, :]
    lane = lanes_of(main.shape)
    tail = roll(side, 104)
    for e in range(1, EVENTS):
        tail = tail + roll(side, 104 - 32 * e)
    both = jnp.where(lane < 112, roll(main, -RIM), tail)
    kinds = zone[pl.ds(0, ROWS // 8, stride=8), :]
    rows = jnp.concatenate([jnp.sum(both[8 * i : 8 * i + 8], axis=0, keepdims=True) for i in range(ROWS // 8)], axis=0)
    parts = [jnp.sum(jnp.where(kinds == k, rows, 0.0), axis=0, keepdims=True) for k in range(ZONES)]
    sums = jnp.sum(jnp.concatenate(parts, axis=0), axis=1, keepdims=True)
    square = (ZONES, LANES)
    row = jnp.sum(jnp.where(rows_of(square) == lanes_of(square), sums, 0.0), axis=0, keepdims=True)
    lane1 = lanes_of(row.shape)
    each = jnp.ones(row.shape, jnp.float32)
    for k in range(ZONES):
        each = jnp.where(lane1 == k, manning[k], each)
    return row * (-2.0 / ALPHA) / each


SUB = 24


def chunks(rows, step, sub=None):
    sub = min(sub or rows, rows)

    def one(i, carry):
        for j in range(0, rows, sub):
            step(pl.multiple_of(BASE + i * rows + j, 8), sub)
        return carry

    lax.fori_loop(0, EXT // rows, one, 0)


CHUNK_F = 144
CHUNK_B = 144
CHUNK_W = 48
CHUNK_A = 72


FULL = ("fx", "fy", "keep_x", "keep_y", "term_x", "term_y", "here_x", "here_y", "next_x", "next_y", "own_x", "own_y")
FULL += ("back_x", "bar_y", "side_y")
PLANE = ("ground", "gbx", "gby", "rough_x", "rough_y", "classes")
NAMES = FULL + PLANE + ("depth", "bar", "side_x", "down_y")
Views = collections.namedtuple("Views", NAMES)


def view_scratch():
    tall = (TALL, LANES)
    shapes = [(STEPS, WIDE) + tall] * len(FULL) + [(2,) + tall] * len(PLANE)
    shapes += [(STEPS + 1, WIDE) + tall] * 2 + [(WIDE,) + tall] * 2
    return [pltpu.VMEM(shape, jnp.float32) for shape in shapes]


def over_steps(low, high, down, run):
    if not LOOP_T:
        for t in reversed(range(low, high)) if down else range(low, high):
            run(t)
        return

    def one(i, carry):
        run(high - 1 - i if down else low + i)
        return carry

    lax.fori_loop(0, high - low, one, 0)


LOOP_T = False


def forward(v):
    chunks(CHUNK_F, lambda r0, n: forward_chunk(True, False, 0, r0, n, v))
    over_steps(1, STEPS, False, lambda t: chunks(CHUNK_F, lambda r0, n: forward_chunk(False, False, t, r0, n, v)))


def backward(v):
    chunks(CHUNK_B, lambda r0, n: backward_chunk(False, True, STEPS - 1, r0, n, v))
    over_steps(1, STEPS - 1, True, lambda t: chunks(CHUNK_B, lambda r0, n: backward_chunk(False, False, t, r0, n, v)))
    chunks(CHUNK_A, lambda r0, n: backward_chunk(True, False, 0, r0, n, v))


def stage_of(which):
    gy, gx, ny, nx = mesh_place()
    return (ny, gy) if which == 0 else (nx, gx)


def stage_peers(which):
    gy, gx, ny, nx = mesh_place()
    if which == 0:
        far = sorted(range(1, ny), key=lambda off: -min(off, ny - off))
        return [(lax.rem(gy + off, ny), gx) for off in far]
    if nx % 32:
        return [(gy, lax.rem(gx + off, nx)) for off in range(1, nx)]
    x, y, core = gx // 8, lax.rem(gx // 2, 4), lax.rem(gx, 2)
    xs = [lax.rem(x + d, nx // 8) * 8 for d in range(nx // 8)]
    ys = [lax.rem(y + d, 4) * 2 for d in range(4)]
    cores = [core, 1 - core]
    hops = lambda d, n: min(d, n - d)
    steps = [(dx, dy, dc) for dx in range(nx // 8) for dy in range(4) for dc in range(2)][1:]
    steps.sort(key=lambda d: -(2 * hops(d[0], nx // 8) + 2 * hops(d[1], 4) + d[2]))
    return [(gy, xs[dx] + ys[dy] + cores[dc]) for dx, dy, dc in steps]


def greet_stage(barrier, which):
    for to in stage_peers(which):
        pl.semaphore_signal(barrier, inc=1, device_id=to, device_id_type=MESH)


def send_stage(which, value, slots, send, recv):
    count, me = stage_of(which)
    slots[me] = value
    for to in stage_peers(which):
        pltpu.make_async_remote_copy(
            src_ref=slots.at[me],
            dst_ref=slots.at[me],
            send_sem=send.at[which],
            recv_sem=recv.at[which],
            device_id=to,
            device_id_type=MESH,
        ).start()


def sum_stage(which, slots, recv):
    count, me = stage_of(which)
    others = slots.at[pl.ds(0, count - 1)]
    pltpu.make_async_copy(others, others, recv.at[which]).wait()
    return jnp.sum(slots[...], axis=0)


def drain_stage(which, slots, send):
    count, me = stage_of(which)
    others = slots.at[pl.ds(0, count - 1)]
    pltpu.make_async_copy(others, others, send.at[which]).wait()


def kernel(
    manning, depth, bed, zone, observe, final, grad, total,
    ext, zone_here, col_left, col_right, msg_left, msg_right, final_here, grad_here, slots_y, slots_x,
    own_sems, rim_send, rim_recv, sum_send, sum_recv, out_sems, *views,
):
    v = Views(*views)
    gy, gx, ny, nx = mesh_place()
    barrier = pltpu.get_barrier_semaphore()
    copies = own_copies(depth, bed, zone, observe, ext, zone_here, own_sems)
    greet_neighbours(barrier)
    for copy in copies:
        copy.start()
    greet_stage(barrier, 0)
    greet_stage(barrier, 1)
    for copy in copies:
        copy.wait()
    fill_rough(manning, zone_here, ext)
    pack_rims(ext, msg_left, msg_right)
    pl.semaphore_wait(barrier, 8 + ny - 1 + nx - 1)
    rims = rim_copies(ext, col_left, col_right, msg_left, msg_right, rim_send, rim_recv)
    for copy in rims:
        copy.start()
    windows_before(ext, v)
    for copy in rims:
        copy.wait()
    windows_after(ext, col_left, col_right, v)
    forward(v)
    backward(v)
    send_stage(0, class_row(manning, zone_here, v.classes), slots_y, sum_send, sum_recv)
    chunks(CHUNK_A, lambda r0, n: start_chunk(r0, n, v))
    unwindow(v.bar.at[0], grad_here, None)
    grad_copy = pltpu.make_async_copy(grad_here, grad, out_sems.at[0])
    grad_copy.start()
    unwindow(v.depth.at[STEPS], final_here, 1.0 / ALPHA)
    final_copy = pltpu.make_async_copy(final_here, final, out_sems.at[1])
    final_copy.start()
    send_stage(1, sum_stage(0, slots_y, sum_recv), slots_x, sum_send, sum_recv)
    grad_copy.wait()
    final_copy.wait()
    drain_stage(0, slots_y, sum_send)
    total[...] = sum_stage(1, slots_x, sum_recv)[0, :ZONES]
    drain_stage(1, slots_x, sum_send)


def vmem():
    return pl.BlockSpec(memory_space=pltpu.VMEM)


def smem():
    return pl.BlockSpec(memory_space=pltpu.SMEM)


def f32(*shape):
    return jax.ShapeDtypeStruct(shape, jnp.float32)


LIMIT = 60 * 1024 * 1024


def finish_kernel(final_here, grad_here, sums_here, final, grad, sums):
    final[...] = final_here[...]
    grad[...] = grad_here[...]
    sums[...] = sums_here[...]


def anywhere():
    return pl.BlockSpec(memory_space=pl.ANY)


def body(depth_start, bed_height, zone_map, manning, observe):
    ny, nx = lax.axis_size("gy"), lax.axis_size("gx")
    block = pltpu.VMEM((ROWS, LANES), jnp.float32)
    blocks = pltpu.VMEM((EVENTS, ROWS, LANES), jnp.float32)
    rim = pltpu.VMEM((EXT, LANES), jnp.float32)
    final, grad, sums = pl.pallas_call(
        kernel,
        out_shape=(f32(EVENTS, ROWS, LANES), f32(EVENTS, ROWS, LANES), f32(ZONES)),
        in_specs=[smem(), anywhere(), anywhere(), anywhere(), anywhere()],
        out_specs=(anywhere(), anywhere(), vmem()),
        scratch_shapes=[
            pltpu.VMEM((10, EXT, LANES), jnp.float32),
            pltpu.VMEM((ROWS, LANES), jnp.int32),
            rim, rim, block, block, blocks, blocks,
            pltpu.VMEM((ny, 1, LANES), jnp.float32),
            pltpu.VMEM((nx, 1, LANES), jnp.float32),
            pltpu.SemaphoreType.DMA((4,)),
            pltpu.SemaphoreType.DMA((8,)),
            pltpu.SemaphoreType.DMA((8,)),
            pltpu.SemaphoreType.DMA((2,)),
            pltpu.SemaphoreType.DMA((2,)),
            pltpu.SemaphoreType.DMA((2,)),
        ]
        + view_scratch(),
        compiler_params=pltpu.CompilerParams(collective_id=0, has_side_effects=True, vmem_limit_bytes=LIMIT),
        name="flood",
    )(manning, depth_start, bed_height, zone_map, observe)
    return pl.pallas_call(
        finish_kernel,
        out_shape=(f32(EVENTS, ROWS, LANES), f32(EVENTS, ROWS, LANES), f32(ZONES)),
        in_specs=[vmem(), vmem(), vmem()],
        out_specs=(vmem(), vmem(), vmem()),
        compiler_params=pltpu.CompilerParams(vmem_limit_bytes=LIMIT),
        name="finish",
    )(final, grad, sums)


def solution(mesh):
    in_specs = (P(None, "gy", "gx"), P("gy", "gx"), P("gy", "gx"), P(), P(None, "gy", "gx"))
    out_specs = (P(None, "gy", "gx"), P(None, "gy", "gx"), P())
    return jax.shard_map(body, mesh=mesh, in_specs=in_specs, out_specs=out_specs, check_vma=False)
```

```python
import collections
import functools

import jax
import jax.numpy as jnp
from jax import lax
from jax.experimental import pallas as pl
from jax.experimental.pallas import tpu as pltpu
from jax.sharding import PartitionSpec as P

STEPS = 4
ZONES = 16
EVENTS = 4
GRAVITY = 9.81
TIME_STEP = 0.3
SPACING = 2.0
CENTRE = 0.7
FLOOR = 0.01

RATE = TIME_STEP / SPACING
SIDE = 0.5 * (1.0 - CENTRE)
MID = CENTRE / SIDE
ALPHA = RATE * GRAVITY * TIME_STEP / (2.0 * SPACING * SIDE)
BETA = RATE * ALPHA
POWER = -7.0 / 3.0
FLOOR_SQ = (BETA * FLOOR) ** 2
ROUGH_SCALE = GRAVITY * TIME_STEP * (2.0 * ALPHA) ** (-POWER) / (BETA * SIDE)
WALL = 1e20

ROWS = 128
LANES = 128
RIM = 8
EXT = ROWS + 2 * RIM
PAD = 8
TALL = EXT + 2 * PAD
BASE = PAD
WIDE = EVENTS + 1

MESH = pl.DeviceIdType.MESH


def lanes_of(shape):
    return lax.broadcasted_iota(jnp.int32, shape, len(shape) - 1)


def rows_of(shape):
    return lax.broadcasted_iota(jnp.int32, shape, len(shape) - 2)


def roll(value, shift, axis=None):
    axis = value.ndim - 1 if axis is None else axis
    return pltpu.roll(value, shift % value.shape[axis], axis)


def mesh_place():
    gy, gx = lax.axis_index("gy"), lax.axis_index("gx")
    ny, nx = lax.axis_size("gy"), lax.axis_size("gx")
    return gy, gx, ny, nx


def own_copies(depth, bed, zone, observe, ext, zone_here, sems):
    own = pl.ds(RIM, ROWS)
    pairs = [
        (zone, zone_here),
        (bed, ext.at[8, own]),
        (depth, ext.at[pl.ds(0, EVENTS), own]),
        (observe, ext.at[pl.ds(EVENTS, EVENTS), own]),
    ]
    return [pltpu.make_async_copy(src, dst, sems.at[i]) for i, (src, dst) in enumerate(pairs)]


def fill_rough(manning, zone, ext):
    classes = zone[pl.ds(0, ROWS // 8, stride=8), :]
    rough = jnp.zeros(classes.shape, jnp.float32)
    for k in range(ZONES):
        m = manning[k]
        rough = jnp.where(classes == k, m * m * ROUGH_SCALE, rough)
    for i in range(ROWS // 8):
        ext[9, RIM + 8 * i : RIM + 8 * i + 8, :] = jnp.broadcast_to(rough[i : i + 1], (8, LANES))


def pack_rims(ext, msg_left, msg_right):
    def one(i, carry):
        here, own = pl.ds(pl.multiple_of(128 * i, 8), 128), pl.ds(pl.multiple_of(128 * i + RIM, 8), 128)
        slot8 = lanes_of((128, LANES)) // 8
        left = jnp.zeros((128, LANES), jnp.float32)
        right = jnp.zeros((128, LANES), jnp.float32)
        for q in range(10):
            value = scaled(q, ext[q, own, :])
            right = jnp.where(slot8 == q, roll(value, 8 * q + 8), right)
            for e in range(EVENTS):
                at = {e: 4 * e + 3, EVENTS + e: 4 * e + 2, 8: 4 * e + 1, 9: 4 * e}.get(q)
                if at is not None:
                    left = jnp.where(slot8 == at, roll(value, 8 * at), left)
        msg_left[here, :] = left
        msg_right[here, :] = right
        return carry

    lax.fori_loop(0, ROWS // 128, one, 0)


def neighbours():
    gy, gx, ny, nx = mesh_place()
    up, down = lax.rem(gy + ny - 1, ny), lax.rem(gy + 1, ny)
    west, east = lax.rem(gx + nx - 1, nx), lax.rem(gx + 1, nx)
    return gy, gx, up, down, west, east


def rim_copies(ext, col_left, col_right, msg_left, msg_right, send, recv):
    gy, gx, up, down, west, east = neighbours()
    plans = [
        (msg_left.at[pl.ds(ROWS - RIM, RIM)], col_right.at[pl.ds(0, RIM)], (down, west)),
        (msg_left.at[pl.ds(0, RIM)], col_right.at[pl.ds(RIM + ROWS, RIM)], (up, west)),
        (msg_right.at[pl.ds(ROWS - RIM, RIM)], col_left.at[pl.ds(0, RIM)], (down, east)),
        (msg_right.at[pl.ds(0, RIM)], col_left.at[pl.ds(RIM + ROWS, RIM)], (up, east)),
        (msg_left, col_right.at[pl.ds(RIM, ROWS)], (gy, west)),
        (msg_right, col_left.at[pl.ds(RIM, ROWS)], (gy, east)),
        (ext.at[:, pl.ds(ROWS, RIM)], ext.at[:, pl.ds(0, RIM)], (down, gx)),
        (ext.at[:, pl.ds(RIM, RIM)], ext.at[:, pl.ds(RIM + ROWS, RIM)], (up, gx)),
    ]
    return [
        pltpu.make_async_remote_copy(
            src_ref=src,
            dst_ref=dst,
            send_sem=send.at[i],
            recv_sem=recv.at[i],
            device_id=to,
            device_id_type=MESH,
        )
        for i, (src, dst, to) in enumerate(plans)
    ]


def greet_neighbours(barrier):
    gy, gx, up, down, west, east = neighbours()
    for to in [
        (down, west),
        (up, west),
        (down, east),
        (up, east),
        (gy, west),
        (gy, east),
        (down, gx),
        (up, gx),
    ]:
        pl.semaphore_signal(barrier, inc=1, device_id=to, device_id_type=MESH)


def scaled(q, value):
    return value * ALPHA if q < EVENTS or q == 8 else value


def window_side(owns):
    lane = lanes_of(owns[0].shape)
    out = roll(owns[0], 24)
    for e in range(1, EVENTS):
        out = jnp.where(lane >= 32 * e, roll(owns[e], 24 + 32 * e), out)
    return out


def own_windows(ext, at):
    value = [scaled(q, ext[q, at, :]) for q in range(10)]
    mains = [roll(x, RIM) for x in value]
    sides = [window_side(x) for x in (value[:EVENTS], value[EVENTS:8], [value[8]] * EVENTS, [value[9]] * EVENTS)]
    return mains + sides


def window_refs(v):
    first, last = v.depth.at[0], v.bar.at[STEPS]
    mains = [first.at[e] for e in range(EVENTS)] + [last.at[e] for e in range(EVENTS)]
    mains += [v.ground.at[0], v.rough_x.at[0]]
    return mains + [first.at[EVENTS], last.at[EVENTS], v.ground.at[1], v.rough_x.at[1]]


def windows_before(ext, v):
    def one(i, carry):
        r0 = pl.multiple_of(128 * i, 8)
        for ref, value in zip(window_refs(v), own_windows(ext, pl.ds(r0 + RIM, 128))):
            ref[pl.ds(r0 + BASE + RIM, 128), :] = value
        return carry

    lax.fori_loop(0, ROWS // 128, one, 0)


def windows_chunk(r0, n, ext, col_left, col_right, v, own):
    gy, gx, ny, nx = mesh_place()
    here, at = pl.ds(r0, n), pl.ds(r0 - BASE, n)
    left, right = col_left[at, :], col_right[at, :]
    refs = window_refs(v)
    values = [ref[here, :] for ref in refs] if own else own_windows(ext, at)
    lane = lanes_of((n, LANES))
    for q in range(10):
        values[q] = jnp.where(lane < RIM, roll(left, -8 * q), values[q])
    tail = lane % 32 >= 24
    for i in range(4):
        values[10 + i] = jnp.where(tail, roll(right, 8 * i), values[10 + i])
    row = rows_of((n, LANES)) + (gy * ROWS - RIM - BASE + r0)
    wall_y = (row < 0) | (row >= ny * ROWS - 1)
    for ref, value in zip(refs[:9] + refs[10:13], values[:9] + values[10:13]):
        ref[here, :] = value
    for w in range(2):
        ground, rough = (values[8], values[9]) if w == 0 else (values[12], values[13])
        column = lane + (gx * LANES - RIM) if w == 0 else lane % 32 + (gx * LANES + 104)
        wall_x = (column < 0) | (column >= nx * LANES - 1)
        v.gbx[w, here, :] = roll(ground, -1) - ground
        v.rough_x[w, here, :] = jnp.where(wall_x, WALL, rough)
        v.rough_y[w, here, :] = jnp.where(wall_y, WALL, rough)
        if own:
            fall(v, w, r0, n - 8)


def fall(v, w, r0, n):
    v.gby[w, pl.ds(r0, n), :] = v.ground[w, pl.ds(r0 + 1, n), :] - v.ground[w, pl.ds(r0, n), :]


def windows_after(ext, col_left, col_right, v):
    windows_chunk(BASE, RIM, ext, col_left, col_right, v, False)
    windows_chunk(BASE + RIM + ROWS, RIM, ext, col_left, col_right, v, False)
    for w in range(2):
        fall(v, w, BASE, RIM)
        fall(v, w, BASE + EXT - 16, 16)


def inverse(x):
    return pl.reciprocal(x, approx=True)


def face(depth, depth_next, gap, flux, sides, rough, first):
    double = depth + depth_next
    slope = (depth_next - depth) + gap
    drive = double * slope
    drag = rough * jnp.exp2(POWER * jnp.log2(double))
    if first:
        drag = drag * (BETA * FLOOR)
        keep = inverse(drag + 1.0 / SIDE)
        new = keep * (-drive)
        term = new * drag
        own = None
    else:
        size = flux * flux + FLOOR_SQ
        drag = drag * lax.rsqrt(size)
        keep = inverse(drag * size + 1.0 / SIDE)
        new = keep * ((MID * flux + sides) - drive)
        drag = new * drag
        term = drag * size
        own = MID - drag * flux
    both = ((-POWER) * term) * inverse(double) - slope
    return new, keep, term, both + double, both - double, own


def forward_chunk(first, last, t, r0, n, v):
    here, above, below = pl.ds(r0, n), pl.ds(r0 - 1, n), pl.ds(r0 + 1, n)
    for k in range(WIDE):
        w = k // EVENTS
        d = v.depth[t, k, here, :]
        if first:
            qx = qy = sx = sy = None
        else:
            qx = v.fx[t - 1, k, here, :]
            qy = v.fy[t - 1, k, here, :]
            sx = roll(qx, 1) + roll(qx, -1)
            sy = v.fy[t - 1, k, above, :] + v.fy[t - 1, k, below, :]
        nx, kx, zx, hx, ex, ox = face(d, roll(d, -1), v.gbx[w, here, :], qx, sx, v.rough_x[w, here, :], first)
        ny, ky, zy, hy, ey, oy = face(d, v.depth[t, k, below, :], v.gby[w, here, :], qy, sy, v.rough_y[w, here, :], first)
        v.fx[t, k, here, :] = nx
        v.fy[t, k, here, :] = ny
        v.keep_x[t, k, here, :] = kx
        v.keep_y[t, k, here, :] = ky
        v.term_x[t, k, here, :] = zx
        v.term_y[t, k, here, :] = zy
        v.here_x[t, k, here, :] = hx
        v.here_y[t, k, here, :] = hy
        v.next_x[t, k, here, :] = ex
        v.next_y[t, k, here, :] = ey
        if not first:
            v.own_x[t, k, here, :] = ox
            v.own_y[t, k, here, :] = oy
        v.depth[t + 1, k, here, :] = d + (roll(nx, 1) - nx) + (v.fy[t, k, above, :] - ny)


def backward_chunk(first, last, t, r0, n, v):
    here, above, below = pl.ds(r0, n), pl.ds(r0 - 1, n), pl.ds(r0 + 1, n)
    sums = [None, None]
    for k in range(WIDE):
        w = k // EVENTS
        bar_d = v.bar[t + 1, k, here, :]
        back_y = v.bar[t + 1, k, below, :] - bar_d
        if last:
            back_x = roll(bar_d, -1) - bar_d
        else:
            back_x = v.back_x[t + 1, k, here, :]
            back_y = back_y + (
                v.bar_y[t + 1, k, here, :] + (v.side_y[t + 1, k, above, :] + v.side_y[t + 1, k, below, :])
            )
        ax = back_x * v.keep_x[t, k, here, :]
        ay = back_y * v.keep_y[t, k, here, :]
        both = ax * v.term_x[t, k, here, :] + ay * v.term_y[t, k, here, :]
        sums[w] = both if sums[w] is None else sums[w] + both
        v.side_y[t, k, here, :] = ay
        if first:
            v.side_x[k, here, :] = ax
            continue
        v.down_y[k, here, :] = ay * v.next_y[t, k, here, :]
        base = (bar_d + ax * v.here_x[t, k, here, :]) + (ay * v.here_y[t, k, here, :] + v.down_y[k, above, :])
        right = ax * v.next_x[t, k, here, :]
        v.bar[t, k, here, :] = base + roll(right, 1)
        v.back_x[t, k, here, :] = (roll(base + ax, -1) + roll(ax - right, 1)) + (
            (right + ax * v.own_x[t, k, here, :]) - base
        )
        v.bar_y[t, k, here, :] = ay * v.own_y[t, k, here, :]
    for w in range(2):
        if last:
            v.classes[w, here, :] = sums[w]
        else:
            v.classes[w, here, :] = v.classes[w, here, :] + sums[w]


def start_chunk(r0, n, v):
    here, above = pl.ds(r0, n), pl.ds(r0 - 1, n)
    for k in range(WIDE):
        ax, ay = v.side_x[k, here, :], v.side_y[0, k, here, :]
        v.down_y[k, here, :] = ay * v.next_y[0, k, here, :]
        v.bar[0, k, here, :] = (
            v.bar[1, k, here, :]
            + (ax * v.here_x[0, k, here, :] + roll(ax * v.next_x[0, k, here, :], 1))
            + (ay * v.here_y[0, k, here, :] + v.down_y[k, above, :])
        )


def unwindow(source, target, scale):
    def one(i, carry):
        at = pl.ds(pl.multiple_of(64 * i, 8), 64)
        here = pl.ds(pl.multiple_of(64 * i, 8) + BASE + RIM, 64)
        side = source[EVENTS, here, :]
        lane = lanes_of(side.shape)
        for e in range(EVENTS):
            own = jnp.where(lane < 112, roll(source[e, here, :], -RIM), roll(side, 104 - 32 * e))
            target[e, at, :] = own if scale is None else own * scale
        return carry

    lax.fori_loop(0, ROWS // 64, one, 0)


def class_row(manning, zone, classes):
    own = pl.ds(BASE + RIM, ROWS)
    main, side = classes[0, own, :], classes[1, own, :]
    lane = lanes_of(main.shape)
    tail = roll(side, 104)
    for e in range(1, EVENTS):
        tail = tail + roll(side, 104 - 32 * e)
    both = jnp.where(lane < 112, roll(main, -RIM), tail)
    kinds = zone[pl.ds(0, ROWS // 8, stride=8), :]
    rows = jnp.concatenate([jnp.sum(both[8 * i : 8 * i + 8], axis=0, keepdims=True) for i in range(ROWS // 8)], axis=0)
    parts = [jnp.sum(jnp.where(kinds == k, rows, 0.0), axis=0, keepdims=True) for k in range(ZONES)]
    sums = jnp.sum(jnp.concatenate(parts, axis=0), axis=1, keepdims=True)
    square = (ZONES, LANES)
    row = jnp.sum(jnp.where(rows_of(square) == lanes_of(square), sums, 0.0), axis=0, keepdims=True)
    lane1 = lanes_of(row.shape)
    each = jnp.ones(row.shape, jnp.float32)
    for k in range(ZONES):
        each = jnp.where(lane1 == k, manning[k], each)
    return row * (-2.0 / ALPHA) / each


SUB = 24


def chunks(rows, step, sub=None):
    sub = min(sub or rows, rows)

    def one(i, carry):
        for j in range(0, rows, sub):
            step(pl.multiple_of(BASE + i * rows + j, 8), sub)
        return carry

    lax.fori_loop(0, EXT // rows, one, 0)


CHUNK_F = 144
CHUNK_B = 144
CHUNK_W = 48
CHUNK_A = 72


FULL = ("fx", "fy", "keep_x", "keep_y", "term_x", "term_y", "here_x", "here_y", "next_x", "next_y", "own_x", "own_y")
FULL += ("back_x", "bar_y", "side_y")
PLANE = ("ground", "gbx", "gby", "rough_x", "rough_y", "classes")
NAMES = FULL + PLANE + ("depth", "bar", "side_x", "down_y")
Views = collections.namedtuple("Views", NAMES)


def view_scratch():
    tall = (TALL, LANES)
    shapes = [(STEPS, WIDE) + tall] * len(FULL) + [(2,) + tall] * len(PLANE)
    shapes += [(STEPS + 1, WIDE) + tall] * 2 + [(WIDE,) + tall] * 2
    return [pltpu.VMEM(shape, jnp.float32) for shape in shapes]


def over_steps(low, high, down, run):
    if not LOOP_T:
        for t in reversed(range(low, high)) if down else range(low, high):
            run(t)
        return

    def one(i, carry):
        run(high - 1 - i if down else low + i)
        return carry

    lax.fori_loop(0, high - low, one, 0)


LOOP_T = False


def forward(v):
    chunks(CHUNK_F, lambda r0, n: forward_chunk(True, False, 0, r0, n, v))
    over_steps(1, STEPS, False, lambda t: chunks(CHUNK_F, lambda r0, n: forward_chunk(False, False, t, r0, n, v)))


def backward(v):
    chunks(CHUNK_B, lambda r0, n: backward_chunk(False, True, STEPS - 1, r0, n, v))
    over_steps(1, STEPS - 1, True, lambda t: chunks(CHUNK_B, lambda r0, n: backward_chunk(False, False, t, r0, n, v)))
    chunks(CHUNK_A, lambda r0, n: backward_chunk(True, False, 0, r0, n, v))


def stage_of(which):
    gy, gx, ny, nx = mesh_place()
    return (ny, gy) if which == 0 else (nx, gx)


def stage_peers(which):
    gy, gx, ny, nx = mesh_place()
    if which == 0:
        far = sorted(range(1, ny), key=lambda off: -min(off, ny - off))
        return [(lax.rem(gy + off, ny), gx) for off in far]
    if nx % 32:
        return [(gy, lax.rem(gx + off, nx)) for off in range(1, nx)]
    x, y, core = gx // 8, lax.rem(gx // 2, 4), lax.rem(gx, 2)
    xs = [lax.rem(x + d, nx // 8) * 8 for d in range(nx // 8)]
    ys = [lax.rem(y + d, 4) * 2 for d in range(4)]
    cores = [core, 1 - core]
    hops = lambda d, n: min(d, n - d)
    steps = [(dx, dy, dc) for dx in range(nx // 8) for dy in range(4) for dc in range(2)][1:]
    steps.sort(key=lambda d: -(2 * hops(d[0], nx // 8) + 2 * hops(d[1], 4) + d[2]))
    return [(gy, xs[dx] + ys[dy] + cores[dc]) for dx, dy, dc in steps]


def greet_stage(barrier, which):
    for to in stage_peers(which):
        pl.semaphore_signal(barrier, inc=1, device_id=to, device_id_type=MESH)


def send_stage(which, value, slots, send, recv):
    count, me = stage_of(which)
    slots[me] = value
    for to in stage_peers(which):
        pltpu.make_async_remote_copy(
            src_ref=slots.at[me],
            dst_ref=slots.at[me],
            send_sem=send.at[which],
            recv_sem=recv.at[which],
            device_id=to,
            device_id_type=MESH,
        ).start()


def sum_stage(which, slots, recv):
    count, me = stage_of(which)
    others = slots.at[pl.ds(0, count - 1)]
    pltpu.make_async_copy(others, others, recv.at[which]).wait()
    return jnp.sum(slots[...], axis=0)


def drain_stage(which, slots, send):
    count, me = stage_of(which)
    others = slots.at[pl.ds(0, count - 1)]
    pltpu.make_async_copy(others, others, send.at[which]).wait()


def kernel(
    manning, depth, bed, zone, observe, final, grad, total,
    ext, zone_here, col_left, col_right, msg_left, msg_right, final_here, grad_here, slots_y, slots_x,
    own_sems, rim_send, rim_recv, sum_send, sum_recv, out_sems, *views,
):
    v = Views(*views)
    gy, gx, ny, nx = mesh_place()
    barrier = pltpu.get_barrier_semaphore()
    copies = own_copies(depth, bed, zone, observe, ext, zone_here, own_sems)
    greet_neighbours(barrier)
    for copy in copies:
        copy.start()
    greet_stage(barrier, 0)
    greet_stage(barrier, 1)
    for copy in copies:
        copy.wait()
    fill_rough(manning, zone_here, ext)
    pack_rims(ext, msg_left, msg_right)
    pl.semaphore_wait(barrier, 8 + ny - 1 + nx - 1)
    rims = rim_copies(ext, col_left, col_right, msg_left, msg_right, rim_send, rim_recv)
    for copy in rims:
        copy.start()
    windows_before(ext, v)
    for copy in rims[4:6]:
        copy.wait()
    windows_chunk(BASE + RIM, ROWS, ext, col_left, col_right, v, True)
    for copy in rims[:4] + rims[6:]:
        copy.wait()
    windows_after(ext, col_left, col_right, v)
    forward(v)
    backward(v)
    send_stage(0, class_row(manning, zone_here, v.classes), slots_y, sum_send, sum_recv)
    chunks(CHUNK_A, lambda r0, n: start_chunk(r0, n, v))
    unwindow(v.bar.at[0], grad_here, None)
    grad_copy = pltpu.make_async_copy(grad_here, grad, out_sems.at[0])
    grad_copy.start()
    unwindow(v.depth.at[STEPS], final_here, 1.0 / ALPHA)
    final_copy = pltpu.make_async_copy(final_here, final, out_sems.at[1])
    final_copy.start()
    send_stage(1, sum_stage(0, slots_y, sum_recv), slots_x, sum_send, sum_recv)
    grad_copy.wait()
    final_copy.wait()
    drain_stage(0, slots_y, sum_send)
    total[...] = sum_stage(1, slots_x, sum_recv)[0, :ZONES]
    drain_stage(1, slots_x, sum_send)


def vmem():
    return pl.BlockSpec(memory_space=pltpu.VMEM)


def smem():
    return pl.BlockSpec(memory_space=pltpu.SMEM)


def f32(*shape):
    return jax.ShapeDtypeStruct(shape, jnp.float32)


LIMIT = 60 * 1024 * 1024


def finish_kernel(final_here, grad_here, sums_here, final, grad, sums):
    final[...] = final_here[...]
    grad[...] = grad_here[...]
    sums[...] = sums_here[...]


def anywhere():
    return pl.BlockSpec(memory_space=pl.ANY)


def body(depth_start, bed_height, zone_map, manning, observe):
    ny, nx = lax.axis_size("gy"), lax.axis_size("gx")
    block = pltpu.VMEM((ROWS, LANES), jnp.float32)
    blocks = pltpu.VMEM((EVENTS, ROWS, LANES), jnp.float32)
    rim = pltpu.VMEM((EXT, LANES), jnp.float32)
    final, grad, sums = pl.pallas_call(
        kernel,
        out_shape=(f32(EVENTS, ROWS, LANES), f32(EVENTS, ROWS, LANES), f32(ZONES)),
        in_specs=[smem(), anywhere(), anywhere(), anywhere(), anywhere()],
        out_specs=(anywhere(), anywhere(), vmem()),
        scratch_shapes=[
            pltpu.VMEM((10, EXT, LANES), jnp.float32),
            pltpu.VMEM((ROWS, LANES), jnp.int32),
            rim, rim, block, block, blocks, blocks,
            pltpu.VMEM((ny, 1, LANES), jnp.float32),
            pltpu.VMEM((nx, 1, LANES), jnp.float32),
            pltpu.SemaphoreType.DMA((4,)),
            pltpu.SemaphoreType.DMA((8,)),
            pltpu.SemaphoreType.DMA((8,)),
            pltpu.SemaphoreType.DMA((2,)),
            pltpu.SemaphoreType.DMA((2,)),
            pltpu.SemaphoreType.DMA((2,)),
        ]
        + view_scratch(),
        compiler_params=pltpu.CompilerParams(collective_id=0, has_side_effects=True, vmem_limit_bytes=LIMIT),
        name="flood",
    )(manning, depth_start, bed_height, zone_map, observe)
    return pl.pallas_call(
        finish_kernel,
        out_shape=(f32(EVENTS, ROWS, LANES), f32(EVENTS, ROWS, LANES), f32(ZONES)),
        in_specs=[vmem(), vmem(), vmem()],
        out_specs=(vmem(), vmem(), vmem()),
        compiler_params=pltpu.CompilerParams(vmem_limit_bytes=LIMIT),
        name="finish",
    )(final, grad, sums)


def solution(mesh):
    in_specs = (P(None, "gy", "gx"), P("gy", "gx"), P("gy", "gx"), P(), P(None, "gy", "gx"))
    out_specs = (P(None, "gy", "gx"), P(None, "gy", "gx"), P())
    return jax.shard_map(body, mesh=mesh, in_specs=in_specs, out_specs=out_specs, check_vma=False)
```
